128 devices in a mesh: wide: 8 (over z, core), narrow: 16 (over x, y).
Axes of the slice: x: 4, y: 4, z: 4, core: 2. Of those that a mesh axis runs over, the one named last changes fastest.
Arguments:
- solution: float32 [512, 256, 128], P(('wide', 'narrow')), may hold values from -6 to 6
- residual: float32 [512, 256, 128], P(('wide', 'narrow')), may hold values from -6 to 6
- direction: float32 [512, 256, 128], P(('wide', 'narrow')), may hold values from -6 to 6
- last_inner: float32 [128], replicated, may hold values from 32768 to 262144
- interface_stiffness_block: bfloat16 [512, 512, 512], P(('wide', 'narrow')), as said below
- cross_conductance: bfloat16 [512, 512, 1152], P(('wide', 'narrow')), may hold values from -0.25 to 0.25
- dirichlet_inverse: bfloat16 [512, 1152, 1152], P(('wide', 'narrow')), as said below
- flux_solve_operator: bfloat16 [512, 512, 512], P(('wide', 'narrow')), as said below
- coarse_shape_functions: bfloat16 [512, 512, 200], P(('wide', 'narrow')), may hold values from -2 to 2
- panels: bfloat16 [512, 200, 200], P(('wide', 'narrow')), as said below
- base_coarse: float32 [8, 256, 256], P('wide'), as said below
- owners: int32 [512, 1], P(('wide', 'narrow')), may hold values from 0 to 7; in each aligned block of 4 rows (0 to 3, 4 to 7, ...) at most 2 rows name the same one
- prim_map: int32 [512, 200], P(('wide', 'narrow')), may hold values from 0 to 255, as said below
- changed: int32 [512], P(('wide', 'narrow')), may hold values 0 or 1
Outputs:
- new_solution: float32 [512, 256, 128], P(('wide', 'narrow'))
- new_residual: float32 [512, 256, 128], P(('wide', 'narrow'))
The draws below stay inside these ranges and needn't reach their ends.
Inputs may be any that keep to these rules, and one draw needn't show every extreme that they name: `owners`: coarse block of each subdomain in column 0; at most 2 of the 4 subdomains of one device name the same block, and some device reaches 2. `prim_map`: the 200 rows of one subdomain are distinct. `interface_stiffness_block`: each block symmetric positive definite. `dirichlet_inverse`: each block symmetric positive definite. `flux_solve_operator`: each block symmetric positive definite. `panels`: each panel symmetric positive definite. `base_coarse`: each block symmetric positive definite.
All inputs are finite; a program needn't handle non-finite values. No bound on the sum of `changed` on one device may be relied on, other than what follows from the above.
Results may differ from the reference program's by a relative error of at most 0.0014.
Values may be sent and summed in bfloat16 or wider, within the bound.
No kernel may reach another device: no remote copies, remote signals or barrier semaphores. Data moves between devices by JAX's collectives and lax.ppermute only.
A program may use at most 128 MiB of HBM per device.

```python
import math
import jax
import jax.numpy as jnp
import numpy as np
from jax import lax

SUB_DEV = 4
NF = 256
NB = 512
NI = 1152
NP = 200
CO = 256
RHS = 128
SUBDOMAINS = 512
COARSE = 8
MOST = 2
N_WIDE = 8
N_NARROW = 16


def dominant(key, leading, order, low, high, spread):
    first, second = jax.random.split(key)
    raw = jax.random.uniform(first, (leading, order, order), jnp.float32, -1.0, 1.0) * (spread / order ** 0.5)
    rows_index = jnp.arange(order)[:, None]
    cols_index = jnp.arange(order)[None, :]
    symmetric = jnp.where(rows_index < cols_index, raw, jnp.swapaxes(raw, 1, 2))
    diagonal = jax.random.uniform(second, (leading, order), jnp.float32, low, high)
    return jnp.where(rows_index == cols_index, diagonal[:, :, None], symmetric)


def draw_interface_stiffness_block(key, part):
    key = jax.random.fold_in(key, 11)
    return dominant(key, SUBDOMAINS, NB, 6.0, 9.0, 3.0).astype(jnp.bfloat16)


def draw_dirichlet_inverse(key, part):
    key = jax.random.fold_in(key, 12)
    return dominant(key, SUBDOMAINS, NI, 0.6, 0.9, 0.3).astype(jnp.bfloat16)


def draw_flux_solve_operator(key, part):
    key = jax.random.fold_in(key, 13)
    return dominant(key, SUBDOMAINS, NB, 0.5, 0.75, 0.25).astype(jnp.bfloat16)


def draw_panels(key, part):
    key = jax.random.fold_in(key, 14)
    return dominant(key, SUBDOMAINS, NP, 1.0, 1.5, 0.5).astype(jnp.bfloat16)


def draw_base_coarse(key, part):
    key = jax.random.fold_in(key, 15)
    return dominant(key, COARSE, CO, 24.0, 36.0, 12.0)


def pick_rows(single_key):
    return jax.random.permutation(single_key, CO)[:NP]


def draw_prim_map(key, part):
    key = jax.random.fold_in(key, 16)
    subdomain_keys = jax.random.split(key, SUBDOMAINS)
    return jax.vmap(pick_rows)(subdomain_keys).astype(jnp.int32)


def with_ends(array, key, least, high):
    longest = array.shape.index(max(array.shape))
    spots = []
    for shift in (0, 1):
        where = [jax.random.randint(jax.random.fold_in(key, axis), (), 0, length) for axis, length in enumerate(array.shape)]
        where[longest] = (where[longest] + shift) % array.shape[longest]
        spots.append(tuple(where))
    return array.at[spots[0]].set(least).at[spots[1]].set(high)


def block_levels(key, dims, cuts, low, top_value):
    factor_of = 1.0
    for axis_at, blocks in cuts:
        steps = jax.random.uniform(jax.random.fold_in(jax.random.fold_in(key, 6), axis_at), (blocks,), jnp.float32, low / len(cuts), top_value / len(cuts))
        factor_of = factor_of * jnp.repeat(jnp.exp(steps), dims[axis_at] // blocks).reshape((-1,) + (1,) * (len(dims) - 1 - axis_at))
    return factor_of


def assign_block(stream_key, own, number, rows, amount, top, limit, lean):
    sequence = jax.random.permutation(stream_key, amount)
    crowded, ordinary = portions_of(amount, rows * top, limit, lean, True), portions_of(amount, rows * top, limit, lean, False)
    places = jnp.arange(amount)

    def named(lengths, rotation):
        used = int((lengths > 0).sum())
        fixed = max(1, used // 4)
        passed = fixed + (places - fixed + rotation * (used - fixed)) % max(1, amount - fixed)
        return jnp.zeros((amount,), jnp.int32).at[sequence[jnp.where(places < fixed, places, passed)]].set(jnp.asarray(lengths, jnp.int32))

    lengths = jnp.where(number % 4 == 0, named(crowded, number // 4), named(ordinary, number - number // 4 - 1))
    mixed = jax.random.permutation(jax.random.fold_in(own, 3), amount)
    donor, receiver = mixed[0:amount // 2 * 2:2], mixed[1:amount // 2 * 2:2]
    room = jnp.minimum(lengths[donor] - 1, limit - lengths[receiver]) // 2
    room = jnp.where((donor == sequence[0]) | (receiver == sequence[0]) | (lengths[receiver] == 0), 0, jnp.maximum(room, 0))
    passed = jax.random.randint(jax.random.fold_in(own, 4), (amount // 2,), 0, 1 << 20) % (room + 1)
    lengths = lengths.at[donor].add(-passed).at[receiver].add(passed)
    members = jnp.searchsorted(jnp.cumsum(lengths), jnp.arange(rows * top), side="right").astype(jnp.int32)
    table = members.reshape(top, rows).T
    table = table[jax.random.permutation(jax.random.fold_in(own, 1), rows)]
    rotation = jax.random.randint(jax.random.fold_in(own, 2), (rows, 1), 0, top)
    return jnp.take_along_axis(table, (jnp.arange(top)[None, :] + rotation) % top, axis=1)


def portions_of(number_of, total, reach, slope, full):
    portions = [(1 << 20) // math.isqrt(standing ** slope) + 1 for standing in range(1, number_of + 1)]
    largest = reach if full else min(reach, max(-(-total // number_of), total * portions[0] // sum(portions)))
    least = 1 if total - largest >= number_of - 1 else 0
    given, spare = [largest] + [least] * (number_of - 1), total - largest - least * (number_of - 1)
    while spare > 0:
        candidates = [i for i in range(1, number_of) if given[i] < largest] or [i for i in range(1, number_of) if given[i] < reach]
        mass, remaining = sum([portions[i] for i in candidates]), spare
        for i in candidates:
            extra = min(reach - given[i], max(1, remaining * portions[i] // mass), spare)
            given[i] = given[i] + extra
            spare = spare - extra
    return np.array(given)


def normal_values(key, shape, width, limit, shards=(), held_as=jnp.bfloat16):
    level = block_levels(key, shape, shards, -0.22, 0.18) if shards else 1.0
    result = jax.random.normal(key, shape, jnp.float32) * width * level
    return jnp.minimum(jnp.maximum(result, -limit), limit).astype(held_as)


def setup_inputs(seed: int = 0) -> dict:
    keys = jax.random.split(jax.random.key(seed), 15)
    solution = normal_values(keys[0], (SUBDOMAINS, NF, RHS), 1.0, 6.0, ((0, 128),), jnp.float32)
    residual = normal_values(keys[1], (SUBDOMAINS, NF, RHS), 1.0, 6.0, ((0, 128),), jnp.float32)
    direction = normal_values(keys[2], (SUBDOMAINS, NF, RHS), 1.0, 6.0, ((0, 128),), jnp.float32)
    last_inner = jnp.clip(jnp.exp(jax.random.uniform(keys[3], (RHS,), jnp.float32, math.log(32768.0), math.log(262144.0))), 32768.0, 262144.0)
    interface_stiffness_block = draw_interface_stiffness_block(jax.random.fold_in(keys[14], 71), 0)
    cross_conductance = normal_values(keys[5], (SUBDOMAINS, NB, NI), (NI // 2) ** -0.5, 0.25, ((0, 128),))
    dirichlet_inverse = draw_dirichlet_inverse(jax.random.fold_in(keys[14], 71), 0)
    flux_solve_operator = draw_flux_solve_operator(jax.random.fold_in(keys[14], 71), 0)
    coarse_shape_functions = normal_values(keys[8], (SUBDOMAINS, NB, NP), (max(NB // 64, 1)) ** -0.5, 2.0, ((0, 128),))
    panels = draw_panels(jax.random.fold_in(keys[14], 71), 0)
    base_coarse = draw_base_coarse(jax.random.fold_in(keys[14], 71), 0)
    owners_keys = jax.random.split(jax.random.fold_in(keys[11], 1), SUBDOMAINS // SUB_DEV)
    owners_turns = jax.random.permutation(jax.random.fold_in(keys[11], 3), SUBDOMAINS // SUB_DEV)
    owners = jax.vmap(lambda own, number: assign_block(jax.random.fold_in(keys[11], 2), own, number, SUB_DEV, COARSE, 1, MOST, 2))(owners_keys, owners_turns).reshape((SUBDOMAINS, 1))
    prim_map = draw_prim_map(jax.random.fold_in(keys[14], 71), 0)
    changed = with_ends((jax.random.randint(keys[13], (SUBDOMAINS,), 0, 2) < 1).astype(jnp.int32), jax.random.fold_in(keys[13], 1), 0, 1)
    return dict(solution=solution, residual=residual, direction=direction, last_inner=last_inner, interface_stiffness_block=interface_stiffness_block, cross_conductance=cross_conductance, dirichlet_inverse=dirichlet_inverse, flux_solve_operator=flux_solve_operator, coarse_shape_functions=coarse_shape_functions, panels=panels, base_coarse=base_coarse, owners=owners, prim_map=prim_map, changed=changed)


def cycle_move(field, offset):
    shaped = field.reshape((N_WIDE, N_NARROW * SUB_DEV) + field.shape[1:])
    return jnp.roll(shaped, offset, axis=1).reshape(field.shape)

def local_view(field):
    return jnp.concatenate([field, cycle_move(field, -1)], axis=1)

def assemble(local_field):
    return local_field[:, :NF] + cycle_move(local_field[:, NF:], 1)

def first_pass(item):
    neumann, basis, subdomain_residual = item
    neumann_part = jnp.dot(neumann.astype(jnp.float32), subdomain_residual.astype(jnp.float32), preferred_element_type=jnp.float32)
    projected = jnp.dot(basis.T.astype(jnp.float32), subdomain_residual.astype(jnp.float32), preferred_element_type=jnp.float32)
    return (neumann_part, projected)

def coarse_pass(item):
    basis, selected_entries = item
    return jnp.dot(basis.astype(jnp.float32), selected_entries.astype(jnp.float32), preferred_element_type=jnp.float32)

def second_pass(item):
    conductance_matrix, linked_product, reciprocal_matrix, local_search_vector = item
    enclosed_source_vector = jnp.dot(linked_product.T.astype(jnp.float32), local_search_vector.astype(jnp.float32), preferred_element_type=jnp.float32).astype(jnp.bfloat16)
    enclosed_heat_values = jnp.dot(reciprocal_matrix.astype(jnp.float32), enclosed_source_vector.astype(jnp.float32), preferred_element_type=jnp.float32).astype(jnp.bfloat16)
    return jnp.dot(conductance_matrix.astype(jnp.float32), local_search_vector.astype(jnp.float32), preferred_element_type=jnp.float32) - jnp.dot(linked_product.astype(jnp.float32), enclosed_heat_values.astype(jnp.float32), preferred_element_type=jnp.float32)

def solve_blocks(matrices, right):
    factors = jnp.linalg.cholesky(matrices)
    return jax.vmap(lambda factor, load: jax.scipy.linalg.cho_solve((factor, True), load))(factors, right)

def reference(solution, residual, direction, last_inner, interface_stiffness_block, cross_conductance, dirichlet_inverse, flux_solve_operator, coarse_shape_functions, panels, base_coarse, owners, prim_map, changed):
    owner_index = owners[:, 0]
    subdomain_residual = local_view(residual.astype(jnp.bfloat16))
    neumann_part, projected = lax.map(first_pass, (flux_solve_operator, coarse_shape_functions, subdomain_residual))
    coarse_rhs = jnp.zeros((COARSE, CO, RHS), jnp.float32).at[owner_index[:, None], prim_map].add(projected)
    weighted_panels = panels.astype(jnp.float32) * changed[:, None, None].astype(jnp.float32)
    added = jnp.zeros((COARSE, CO, CO), jnp.float32).at[owner_index[:, None, None], prim_map[:, :, None], prim_map[:, None, :]].add(weighted_panels)
    coarse_solution = solve_blocks(base_coarse + added, coarse_rhs).astype(jnp.bfloat16)
    selected_entries = coarse_solution[owner_index[:, None], prim_map]
    precond_local = neumann_part + lax.map(coarse_pass, (coarse_shape_functions, selected_entries))
    precond = 0.5 * assemble(precond_local)
    inner = jnp.sum(residual * precond, axis=(0, 1))
    search = precond + inner / last_inner * direction
    local_search_vector = local_view(search.astype(jnp.bfloat16))
    image_local = lax.map(second_pass, (interface_stiffness_block, cross_conductance, dirichlet_inverse, local_search_vector))
    image = assemble(image_local)
    curvature = jnp.sum(search * image, axis=(0, 1))
    step_size = inner / curvature
    return (solution + step_size * search, residual - step_size * image)
```

```python
import jax
import jax.numpy as jnp
from jax import lax
from jax.experimental import pallas as pl
from jax.experimental.pallas import tpu as pltpu
from jax.sharding import Mesh, PartitionSpec as P

F32 = jnp.float32
BF16 = jnp.bfloat16
NN = (((1,), (0,)), ((), ()))
NT = (((1,), (1,)), ((), ()))
TN = (((0,), (0,)), ((), ()))
LIMIT = 24 * 1024 * 1024


def dot(a, b, dims=NN, precision=None):
    return lax.dot_general(a, b, dims, precision=precision, preferred_element_type=F32)


def smem():
    return pl.BlockSpec(memory_space=pltpu.SMEM)


def whole(shape):
    return pl.BlockSpec(shape, lambda *_: (0,) * len(shape))


def params(*semantics):
    return pltpu.CompilerParams(vmem_limit_bytes=LIMIT)


def place_kernel(own, chg, core, pm, basis, panel, res, keep, send, spread):
    s = pl.program_id(0)
    co = spread.shape[2]
    half = co // 2
    face = res.shape[1]

    @pl.when(s == 0)
    def _():
        keep[...] = jnp.zeros_like(keep)
        send[...] = jnp.zeros_like(send)

    rows = lax.broadcasted_iota(jnp.int32, (co, pm.shape[2]), 0)
    select = (rows == pm[0]).astype(F32).astype(BF16)
    wide_basis = dot(basis[0], select, NT).astype(BF16)
    spread[0] = wide_basis
    placed = dot(dot(select, panel[0]).astype(BF16), select, NT) * chg[s].astype(F32)
    last = pl.num_programs(0) - 1
    here = res[s].astype(BF16)
    there = res[jnp.minimum(s + 1, last)].astype(BF16)
    rhs = dot(wide_basis[:face], here, TN)
    rhs += jnp.where(s < last, dot(wide_basis[face:], there, TN), 0.0)
    owner = own[s]
    place = owner >> 1
    other = (owner & 1) != core[0]

    def add(to):
        to[place, 0:half] += placed[:half, :half]
        to[place, half:co] += placed[half:, :half]
        to[place, co : co + half] += placed[half:, half:]
        to[place, co + half :] += rhs

    @pl.when(other)
    def _():
        add(send)

    @pl.when(jnp.logical_not(other))
    def _():
        add(keep)


def place_panels(own, chg, core, prim_map, basis, panels, residual, groups):
    subs, nb, npr = basis.shape
    co = 2 * residual.shape[2]
    rows = 3 * (co // 2) + co
    packed = (groups, rows, co // 2)
    return pl.pallas_call(
        place_kernel,
        grid=(subs,),
        in_specs=[
            smem(),
            smem(),
            smem(),
            pl.BlockSpec((1, 1, npr), lambda s: (s, 0, 0)),
            pl.BlockSpec((1, nb, npr), lambda s: (s, 0, 0)),
            pl.BlockSpec((1, npr, npr), lambda s: (s, 0, 0)),
            whole(residual.shape),
        ],
        out_specs=[whole(packed), whole(packed), pl.BlockSpec((1, nb, co), lambda s: (s, 0, 0))],
        out_shape=[
            jax.ShapeDtypeStruct(packed, F32),
            jax.ShapeDtypeStruct(packed, F32),
            jax.ShapeDtypeStruct((subs, nb, co), BF16),
        ],
        compiler_params=params(),
        cost_estimate=pl.CostEstimate(flops=10**9, bytes_accessed=6 * 10**6, transcendentals=0),
        name="place_panels",
    )(own, chg, core, prim_map, basis, panels, residual)


def halo_kernel(own, core, spread, halo, keep_in, send_in, keep, send, held, sem):
    del keep_in, send_in
    owner = own[own.shape[0] - 1]
    place = owner >> 1
    other = (owner & 1) != core[0]
    rows = held.shape[0]

    def add(to):
        part = to.at[place, pl.ds(to.shape[1] - rows, rows)]
        fetch = pltpu.make_async_copy(part, held, sem)
        fetch.start()
        value = dot(spread[0], halo[...], TN)
        fetch.wait()
        held[...] += value
        put = pltpu.make_async_copy(held, part, sem)
        put.start()
        put.wait()

    @pl.when(other)
    def _():
        add(send)

    @pl.when(jnp.logical_not(other))
    def _():
        add(keep)


def add_halo(own, core, spread, halo, keep, send):
    subs, nb, co = spread.shape
    hbm = pl.BlockSpec(memory_space=pl.ANY)
    return pl.pallas_call(
        halo_kernel,
        grid=(1,),
        in_specs=[
            smem(),
            smem(),
            pl.BlockSpec((1, nb // 2, co), lambda _: (subs - 1, 1, 0)),
            whole(halo.shape),
            hbm,
            hbm,
        ],
        out_specs=[hbm, hbm],
        out_shape=[jax.ShapeDtypeStruct(keep.shape, F32), jax.ShapeDtypeStruct(send.shape, F32)],
        input_output_aliases={4: 0, 5: 1},
        scratch_shapes=[pltpu.VMEM((co, halo.shape[1]), F32), pltpu.SemaphoreType.DMA],
        compiler_params=params(),
        name="add_halo",
    )(own, core, spread, halo, keep, send)


def inverse(matrix):
    n = matrix.shape[0]
    lanes = lax.broadcasted_iota(jnp.int32, (8, n), 1)
    subl = lax.broadcasted_iota(jnp.int32, (8, n), 0)
    tiles = tuple(matrix[8 * i : 8 * i + 8] for i in range(n // 8))

    def group(_, tiles):
        tiles = list(tiles)
        for j in range(8):
            pivot_row = tiles[0][j : j + 1, :]
            scale = 1.0 / pivot_row[:, j : j + 1]
            row = jnp.where(lanes[:1] == j, scale, pivot_row * scale)
            for i, tile in enumerate(tiles):
                new = jnp.where(lanes == j, 0.0, tile) - tile[:, j : j + 1] * row
                if i == 0:
                    new = jnp.where(subl == j, row, new)
                tiles[i] = new
        return tuple(pltpu.roll(tile, n - 8, 1) for tile in tiles[1:] + tiles[:1])

    return jnp.concatenate(lax.fori_loop(0, n // 8, group, tiles), axis=0)


def solve_kernel(packed, base, out):
    co = out.shape[0]
    half = co // 2
    high = lax.Precision.HIGHEST
    a11 = packed[0:half] + base[0, :half, :half]
    a21 = packed[half:co] + base[0, half:, :half]
    a22 = packed[co : co + half] + base[0, half:, half:]
    b1 = packed[co + half : 2 * co]
    b2 = packed[2 * co :]
    inv1 = inverse(a11)
    carry = dot(a21, inv1, NN, high)
    inv2 = inverse(a22 - dot(carry, a21, NT, high))
    x2 = dot(inv2, b2 - dot(carry, b1, NN, high), NN, high)
    x1 = dot(inv1, b1, NN, high) - dot(carry, x2, TN, high)
    out[:half] = x1.astype(BF16)
    out[half:] = x2.astype(BF16)


def solve_block(packed, base):
    co = base.shape[1]
    return pl.pallas_call(
        solve_kernel,
        out_shape=jax.ShapeDtypeStruct((co, packed.shape[1]), BF16),
        compiler_params=params(),
        name="solve_block",
    )(packed, base)


def neumann_kernel(neumann, res, halo, out):
    s = pl.program_id(0)
    last = pl.num_programs(0) - 1
    here = res[s].astype(BF16)
    there = jnp.where(s < last, res[jnp.minimum(s + 1, last)], halo[...].astype(F32)).astype(BF16)
    out[0] = 0.5 * dot(neumann[0], jnp.concatenate([here, there], axis=0))


def neumann_half(neumann, residual, halo):
    subs, nb, _ = neumann.shape
    rhs = residual.shape[2]
    return pl.pallas_call(
        neumann_kernel,
        grid=(subs,),
        in_specs=[
            pl.BlockSpec((1, nb, nb), lambda s: (s, 0, 0)),
            whole(residual.shape),
            whole(halo.shape),
        ],
        out_specs=pl.BlockSpec((1, nb, rhs), lambda s: (s, 0, 0)),
        out_shape=jax.ShapeDtypeStruct((subs, nb, rhs), F32),
        compiler_params=params(),
        cost_estimate=pl.CostEstimate(
            flops=2 * subs * nb * nb * rhs, bytes_accessed=4 * 10**6, transcendentals=0
        ),
        name="neumann_half",
    )(neumann, residual, halo)


def coarse_kernel(own, spread, solved, part, out):
    s = pl.program_id(0)
    out[0] = part[0] + 0.5 * dot(spread[0], solved[own[s]])


def coarse_part(own, spread, solved, part):
    subs, nb, co = spread.shape
    rhs = solved.shape[2]
    return pl.pallas_call(
        coarse_kernel,
        grid=(subs,),
        in_specs=[
            smem(),
            pl.BlockSpec((1, nb, co), lambda s: (s, 0, 0)),
            whole(solved.shape),
            pl.BlockSpec((1, nb, rhs), lambda s: (s, 0, 0)),
        ],
        out_specs=pl.BlockSpec((1, nb, rhs), lambda s: (s, 0, 0)),
        out_shape=jax.ShapeDtypeStruct((subs, nb, rhs), F32),
        compiler_params=params(),
        name="coarse_part",
    )(own, spread, solved, part)


def action(stiffness, coupling, interior, field):
    load = dot(coupling, field, TN).astype(BF16)
    inside = dot(interior, load).astype(BF16)
    return dot(stiffness, field) - dot(coupling, inside)


def operators(nb, ni, place):
    return [
        pl.BlockSpec((1, nb, nb), place),
        pl.BlockSpec((1, nb, ni), place),
        pl.BlockSpec((1, ni, ni), place),
    ]


def cost(steps, nb, ni, rhs):
    return pl.CostEstimate(
        flops=2 * steps * rhs * (nb * nb + 2 * nb * ni + ni * ni),
        bytes_accessed=2 * steps * (nb * nb + nb * ni + ni * ni),
        transcendentals=0,
    )


def direction_kernel(stiffness, coupling, interior, direction, halo, out):
    s = pl.program_id(0)
    last = pl.num_programs(0) - 1
    there = jnp.where(s < last, direction[jnp.minimum(s + 1, last)], halo[...])
    field = jnp.concatenate([direction[s], there], axis=0).astype(BF16)
    out[0] = action(stiffness[0], coupling[0], interior[0], field)


def direction_action(stiffness, coupling, interior, direction, halo):
    subs, nb, ni = coupling.shape
    rhs = direction.shape[2]
    return pl.pallas_call(
        direction_kernel,
        grid=(subs,),
        in_specs=operators(nb, ni, lambda s: (s, 0, 0)) + [whole(direction.shape), whole(halo.shape)],
        out_specs=pl.BlockSpec((1, nb, rhs), lambda s: (s, 0, 0)),
        out_shape=jax.ShapeDtypeStruct((subs, nb, rhs), F32),
        compiler_params=params(),
        cost_estimate=cost(subs, nb, ni, rhs),
        name="direction_action",
    )(stiffness, coupling, interior, direction, halo)


def column_sum(value):
    return jnp.sum(value, axis=0, keepdims=True)


def products(out, sums, image, own_p, far_p, own_d, far_d, own_r, moved_d, first, earlier):
    face = own_p.shape[0]
    out[0] = image
    parts = jnp.concatenate(
        [
            column_sum(own_r * own_p),
            column_sum(own_p * image[:face] + far_p * image[face:]),
            column_sum(own_p * moved_d[:face] + far_p * moved_d[face:])
            + column_sum(own_d * image[:face] + far_d * image[face:]),
            column_sum(own_d * moved_d[:face] + far_d * moved_d[face:]),
        ],
        axis=0,
    )

    @pl.when(first)
    def _():
        sums[...] = earlier + parts

    @pl.when(jnp.logical_not(first))
    def _():
        sums[...] += parts


def inner_kernel(stiffness, coupling, interior, pre, direction, residual, moved, out, sums):
    i = pl.program_id(0)
    s = i + 1
    face = direction.shape[1]
    own_p = pre[s, :face] + pre[s - 1, face:]
    far_p = pre[s + 1, :face] + pre[s, face:]
    field = jnp.concatenate([own_p, far_p], axis=0).astype(BF16)
    image = action(stiffness[0], coupling[0], interior[0], field)
    products(
        out, sums, image, own_p, far_p, direction[s], direction[s + 1], residual[s], moved[s], i == 0, 0.0
    )


def outer_kernel(
    stiffness,
    coupling,
    interior,
    pre,
    from_prev,
    from_next,
    direction,
    direction_halo,
    residual,
    moved,
    earlier,
    out,
    sums,
):
    i = pl.program_id(0)
    last = direction.shape[0] - 1
    s = i * last
    near = jnp.minimum(s + 1, last)
    behind = jnp.maximum(s - 1, 0)
    face = direction.shape[1]
    own_p = pre[s, :face] + jnp.where(i == 0, from_prev[...], pre[behind, face:])
    far_p = pre[s, face:] + jnp.where(i == 0, pre[near, :face], from_next[...])
    far_d = jnp.where(i == 0, direction[near], direction_halo[...])
    field = jnp.concatenate([own_p, far_p], axis=0).astype(BF16)
    image = action(stiffness[0], coupling[0], interior[0], field)
    products(
        out, sums, image, own_p, far_p, direction[s], far_d, residual[s], moved[s], i == 0, earlier[...]
    )


def search_action(kernel, place, steps, stiffness, coupling, interior, *rest):
    _, nb, ni = coupling.shape
    rhs = rest[0].shape[2]
    return pl.pallas_call(
        kernel,
        grid=(steps,),
        in_specs=operators(nb, ni, place) + [whole(x.shape) for x in rest],
        out_specs=[pl.BlockSpec((1, nb, rhs), lambda i: (i, 0, 0)), whole((4, rhs))],
        out_shape=[
            jax.ShapeDtypeStruct((steps, nb, rhs), F32),
            jax.ShapeDtypeStruct((4, rhs), F32),
        ],
        compiler_params=params(),
        cost_estimate=cost(steps, nb, ni, rhs),
        name="search_action",
    )(stiffness, coupling, interior, *rest)


def update_kernel(
    sums, last_inner, pre, from_prev, outer, inside, moved, far, direction, residual, solution, new_sol, new_res
):
    total = jnp.sum(sums[...], axis=0)
    inner = total[0:1]
    beta = inner / last_inner[...]
    curvature = total[1:2] + beta * (total[2:3] + beta * total[3:4])
    step = inner / curvature
    face = direction.shape[1]
    last = direction.shape[0] - 1

    def part(s):
        return outer[0] if s == 0 else outer[1] if s == last else inside[s - 1]

    for s in range(last + 1):
        if s == 0:
            p = pre[s, :face] + from_prev[...]
            image = part(s)[:face] + far[0] + beta * (moved[s, :face] + far[1])
        else:
            p = pre[s, :face] + pre[s - 1, face:]
            image = part(s)[:face] + part(s - 1)[face:] + beta * (moved[s, :face] + moved[s - 1, face:])
        search = p + beta * direction[s]
        new_sol[s] = solution[s] + step * search
        new_res[s] = residual[s] - step * image


def update(*args):
    shape = jax.ShapeDtypeStruct(args[-1].shape, F32)
    return pl.pallas_call(
        update_kernel, out_shape=[shape, shape], compiler_params=params(), name="update"
    )(*args)


def local(
    solution,
    residual,
    direction,
    last_inner,
    stiffness,
    coupling,
    interior,
    neumann,
    basis,
    panels,
    base_coarse,
    owners,
    prim_map,
    changed,
):
    groups = lax.axis_size("z")
    pieces = lax.axis_size("narrow")
    devices = groups * 2 * pieces
    face, rhs = residual.shape[1:]
    forward = [(i, (i + 1) % pieces) for i in range(pieces)]
    back = [((i + 1) % pieces, i) for i in range(pieces)]
    own = owners[:, 0]
    core = lax.axis_index("core")
    core_ref = core.astype(jnp.int32).reshape(1)

    halo = lax.ppermute(residual[0].astype(BF16), "narrow", back)
    keep, send, spread = place_panels(
        own, changed, core_ref, prim_map[:, None, :], basis, panels, residual, groups
    )
    keep, send = add_halo(own, core_ref, spread, halo, keep, send)
    face_d, _ = lax.optimization_barrier((direction[0], halo))
    direction_halo = lax.ppermute(face_d, "narrow", back)
    mine = keep + lax.ppermute(send, "core", [(0, 1), (1, 0)])
    rows = mine.shape[1] // pieces
    parts = lax.all_to_all(
        mine.reshape(groups * pieces, rows, rhs), ("z", "narrow"), 0, 0, tiled=True
    )
    piece = jnp.sum(parts, axis=0)
    packed = lax.all_to_all(
        jnp.broadcast_to(piece[None], (pieces,) + piece.shape), "narrow", 0, 0, tiled=True
    )
    solved = solve_block(packed.reshape(pieces * rows, rhs), base_coarse)

    turns = [lax.ppermute(solved, "z", [(i, (i + d) % groups) for i in range(groups)]) for d in range(1, groups)]
    ring = jnp.stack([solved] + turns)
    twin = lax.ppermute(ring, "core", [(0, 1), (1, 0)])
    pairs = jnp.stack([ring, twin]).reshape((2 * groups,) + solved.shape)
    z = lax.axis_index("z")
    where = ((own & 1) != core) * groups + (z - (own >> 1)) % groups

    part = neumann_half(neumann, residual, halo)
    moved = direction_action(stiffness, coupling, interior, direction, direction_halo)
    pre = coarse_part(where.astype(jnp.int32), spread, pairs, part)
    from_prev = lax.ppermute(pre[-1, face:], "narrow", forward)
    from_next = lax.ppermute(pre[0, :face], "narrow", back)
    inside, sums = search_action(
        inner_kernel, lambda i: (i + 1, 0, 0), 2, stiffness, coupling, interior, pre, direction, residual, moved
    )
    last = residual.shape[0] - 1
    outer, sums = search_action(
        outer_kernel,
        lambda i: (last * i, 0, 0),
        2,
        stiffness,
        coupling,
        interior,
        pre,
        from_prev,
        from_next,
        direction,
        direction_halo,
        residual,
        moved,
        sums,
    )
    far = lax.ppermute(jnp.stack([outer[-1, face:], moved[-1, face:]]), "narrow", forward)
    sums = lax.all_to_all(
        jnp.broadcast_to(sums[None], (devices,) + sums.shape), ("z", "core", "narrow"), 0, 0, tiled=True
    )
    return tuple(
        update(
            sums,
            last_inner[None],
            pre,
            from_prev,
            outer,
            inside,
            moved,
            far,
            direction,
            residual,
            solution,
        )
    )


def solution(mesh):
    wide, narrow = mesh.devices.shape
    finer = Mesh(mesh.devices.reshape(wide // 2, 2, narrow), ("z", "core", "narrow"))
    split = ("z", "core", "narrow")
    in_specs = (
        P(split, None, None),
        P(split, None, None),
        P(split, None, None),
        P(),
        P(split, None, None),
        P(split, None, None),
        P(split, None, None),
        P(split, None, None),
        P(split, None, None),
        P(split, None, None),
        P(("z", "core"), None, None),
        P(split, None),
        P(split, None),
        P(split),
    )
    out_specs = (P(split, None, None), P(split, None, None))
    return jax.shard_map(local, mesh=finer, in_specs=in_specs, out_specs=out_specs, check_vma=False)
```

```python
import jax
import jax.numpy as jnp
from jax import lax
from jax.experimental import pallas as pl
from jax.experimental.pallas import tpu as pltpu
from jax.sharding import Mesh, PartitionSpec as P

F32 = jnp.float32
BF16 = jnp.bfloat16
NN = (((1,), (0,)), ((), ()))
NT = (((1,), (1,)), ((), ()))
TN = (((0,), (0,)), ((), ()))
SMALL = 16 * 1024 * 1024
LARGE = 24 * 1024 * 1024
HIGHEST = lax.Precision.HIGHEST


def dot(a, b, dims=NN, precision=None):
    return lax.dot_general(a, b, dims, precision=precision, preferred_element_type=F32)


def smem():
    return pl.BlockSpec(memory_space=pltpu.SMEM)


def whole(shape):
    return pl.BlockSpec(shape, lambda *_: (0,) * len(shape))


def params(limit=SMALL):
    return pltpu.CompilerParams(vmem_limit_bytes=limit)


def column_sum(value):
    return jnp.sum(value, axis=0, keepdims=True)


def place_kernel(own, chg, core, pm, basis, panel, res, keep, send, spread):
    s = pl.program_id(0)
    co = spread.shape[1]
    half = co // 2
    face = res.shape[1]

    @pl.when(s == 0)
    def _():
        keep[...] = jnp.zeros_like(keep)
        send[...] = jnp.zeros_like(send)

    rows = lax.broadcasted_iota(jnp.int32, (co, pm.shape[2]), 0)
    select = (rows == pm[0]).astype(F32).astype(BF16)
    wide_basis = dot(select, basis[0]).astype(BF16)
    spread[0] = wide_basis
    placed = dot(dot(select, panel[0]).astype(BF16), select, NT) * chg[s].astype(F32)
    last = pl.num_programs(0) - 1
    here = res[s].astype(BF16)
    there = res[jnp.minimum(s + 1, last)].astype(BF16)
    rhs = dot(wide_basis[:, :face], here)
    rhs += jnp.where(s < last, dot(wide_basis[:, face:], there), 0.0)
    owner = own[s]
    place = owner >> 1
    other = (owner & 1) != core[0]

    def add(to):
        to[place, 0:half] += placed[:half, :half]
        to[place, half:co] += placed[half:, :half]
        to[place, co : co + half] += placed[half:, half:]
        to[place, co + half :] += rhs

    @pl.when(other)
    def _():
        add(send)

    @pl.when(jnp.logical_not(other))
    def _():
        add(keep)


def place_panels(own, chg, core, prim_map, basis, panels, residual, groups):
    subs, npr, nb = basis.shape
    co = 2 * residual.shape[2]
    rows = 3 * (co // 2) + co
    packed = (groups, rows, co // 2)
    return pl.pallas_call(
        place_kernel,
        grid=(subs,),
        in_specs=[
            smem(),
            smem(),
            smem(),
            pl.BlockSpec((1, 1, npr), lambda s: (s, 0, 0)),
            pl.BlockSpec((1, npr, nb), lambda s: (s, 0, 0)),
            pl.BlockSpec((1, npr, npr), lambda s: (s, 0, 0)),
            whole(residual.shape),
        ],
        out_specs=[whole(packed), whole(packed), pl.BlockSpec((1, co, nb), lambda s: (s, 0, 0))],
        out_shape=[
            jax.ShapeDtypeStruct(packed, F32),
            jax.ShapeDtypeStruct(packed, F32),
            jax.ShapeDtypeStruct((subs, co, nb), BF16),
        ],
        compiler_params=params(),
        cost_estimate=pl.CostEstimate(flops=10**9, bytes_accessed=6 * 10**6, transcendentals=0),
        name="place_panels",
    )(own, chg, core, prim_map, basis, panels, residual)


def halo_kernel(own, core, spread, halo, keep_in, send_in, keep, send, held, sem):
    del keep_in, send_in
    owner = own[own.shape[0] - 1]
    place = owner >> 1
    other = (owner & 1) != core[0]
    rows = held.shape[0]

    def add(to):
        part = to.at[place, pl.ds(to.shape[1] - rows, rows)]
        fetch = pltpu.make_async_copy(part, held, sem)
        fetch.start()
        value = dot(spread[0], halo[...])
        fetch.wait()
        held[...] += value
        put = pltpu.make_async_copy(held, part, sem)
        put.start()
        put.wait()

    @pl.when(other)
    def _():
        add(send)

    @pl.when(jnp.logical_not(other))
    def _():
        add(keep)


def add_halo(own, core, spread, halo, keep, send):
    subs, co, nb = spread.shape
    hbm = pl.BlockSpec(memory_space=pl.ANY)
    return pl.pallas_call(
        halo_kernel,
        grid=(1,),
        in_specs=[
            smem(),
            smem(),
            pl.BlockSpec((1, co, nb // 2), lambda _: (subs - 1, 0, 1)),
            whole(halo.shape),
            hbm,
            hbm,
        ],
        out_specs=[hbm, hbm],
        out_shape=[jax.ShapeDtypeStruct(keep.shape, F32), jax.ShapeDtypeStruct(send.shape, F32)],
        input_output_aliases={4: 0, 5: 1},
        scratch_shapes=[pltpu.VMEM((co, halo.shape[1]), F32), pltpu.SemaphoreType.DMA],
        compiler_params=params(),
        name="add_halo",
    )(own, core, spread, halo, keep, send)


def gather_kernel(parts, out):
    total = jnp.sum(parts[...], axis=0)
    for i in range(out.shape[0]):
        out[i] = total


def sum_copies(parts, copies):
    return pl.pallas_call(
        gather_kernel,
        out_shape=jax.ShapeDtypeStruct((copies,) + parts.shape[1:], F32),
        compiler_params=params(),
        name="sum_copies",
    )(parts)


MOST_STEPS = 24


def inverse(matrix):
    n = matrix.shape[0]
    lanes = lax.broadcasted_iota(jnp.int32, (8, n), 1)
    subl = lax.broadcasted_iota(jnp.int32, (8, n), 0)
    tiles = tuple(matrix[8 * i : 8 * i + 8] for i in range(n // 8))

    def group(_, tiles):
        tiles = list(tiles)
        for j in range(8):
            pivot_row = tiles[0][j : j + 1, :]
            scale = 1.0 / pivot_row[:, j : j + 1]
            row = jnp.where(lanes[:1] == j, scale, pivot_row * scale)
            for i, tile in enumerate(tiles):
                new = jnp.where(lanes == j, 0.0, tile) - tile[:, j : j + 1] * row
                if i == 0:
                    new = jnp.where(subl == j, row, new)
                tiles[i] = new
        return tuple(pltpu.roll(tile, n - 8, 1) for tile in tiles[1:] + tiles[:1])

    return jnp.concatenate(lax.fori_loop(0, n // 8, group, tiles), axis=0)


def split(value, terms):
    found = []
    for _ in range(terms):
        found.append(value.astype(BF16))
        value = value - found[-1].astype(F32)
    return found


def eliminate(matrix, right):
    half = matrix.shape[0] // 2
    a21 = matrix[half:, :half]
    b1, b2 = right[:half], right[half:]
    inv1 = inverse(matrix[:half, :half])
    carry = dot(a21, inv1, NN, HIGHEST)
    inv2 = inverse(matrix[half:, half:] - dot(carry, a21, NT, HIGHEST))
    x2 = dot(inv2, b2 - dot(carry, b1, NN, HIGHEST), NN, HIGHEST)
    x1 = dot(inv1, b1, NN, HIGHEST) - dot(carry, x2, TN, HIGHEST)
    return x1, x2


def solve_kernel(packed, base, out, mat, terms, x, r, p):
    co = out.shape[0]
    half = co // 2
    a21 = packed[half:co]
    mat[:half, :half] = packed[:half] + base[0, :half, :half]
    mat[half:, :half] = a21 + base[0, half:, :half]
    mat[:half, half:] = a21.T + base[0, :half, half:]
    mat[half:, half:] = packed[co : co + half] + base[0, half:, half:]
    rows = lax.broadcasted_iota(jnp.int32, (co, co), 0)
    columns = lax.broadcasted_iota(jnp.int32, (co, co), 1)
    scale = 1.0 / jnp.sum(jnp.where(rows == columns, mat[...], 0.0), axis=1, keepdims=True)
    for i, term in enumerate(split(mat[...], 3)):
        terms[i] = term
    right = packed[co + half :]
    size = jnp.max(jnp.abs(right), axis=0, keepdims=True)
    size = jnp.where(size > 0.0, size, 1.0)
    right = right * (1.0 / size)

    def times(value):
        n = value.shape[1]
        v1, v2, v3 = split(value, 3)
        pair = jnp.concatenate([v1, v2], axis=1)
        first = dot(terms[0], pair)
        second = dot(terms[1], pair)
        small = second[:, n:] + dot(terms[0], v3) + dot(terms[2], v1)
        return first[:, :n] + (first[:, n:] + second[:, :n] + small)

    x[...] = jnp.zeros_like(right)
    r[...] = right
    p[...] = scale * right
    start = column_sum(right * (scale * right))

    def steps(state):
        count, norm, _ = state
        for _ in range(2):
            image = times(p[...])
            energy = column_sum(p[...] * image)
            length = jnp.where(energy > 0.0, norm / energy, 0.0)
            x[...] += length * p[...]
            left = r[...] - length * image
            r[...] = left
            scaled = scale * left
            new = column_sum(left * scaled)
            p[...] = scaled + jnp.where(norm > 0.0, new / norm, 0.0) * p[...]
            norm = new
        return count + 2, norm, jnp.max(norm - 1e-13 * start) > 0.0

    lax.while_loop(
        lambda state: state[2] & (state[0] < MOST_STEPS), steps, (jnp.int32(0), start, jnp.bool_(True))
    )
    left = right - dot(mat[...], x[...], NN, HIGHEST)
    solved = jnp.max(column_sum(left * (scale * left)) - 1e-11 * start) <= 0.0

    @pl.when(solved)
    def _():
        out[...] = (x[...] * size).astype(BF16)

    @pl.when(jnp.logical_not(solved))
    def _():
        x1, x2 = eliminate(mat[...], packed[co + half :])
        out[:half] = x1.astype(BF16)
        out[half:] = x2.astype(BF16)


def solve_block(packed, base):
    co = base.shape[1]
    rhs = packed.shape[1]
    return pl.pallas_call(
        solve_kernel,
        out_shape=jax.ShapeDtypeStruct((co, rhs), BF16),
        scratch_shapes=[
            pltpu.VMEM((co, co), F32),
            pltpu.VMEM((3, co, co), BF16),
            pltpu.VMEM((co, rhs), F32),
            pltpu.VMEM((co, rhs), F32),
            pltpu.VMEM((co, rhs), F32),
        ],
        compiler_params=params(),
        name="solve_block",
    )(packed, base)


def neumann_kernel(neumann, spread, res, halo, out, turned):
    s = pl.program_id(0)
    last = pl.num_programs(0) - 1
    here = res[s].astype(BF16)
    there = jnp.where(s < last, res[jnp.minimum(s + 1, last)], halo[...].astype(F32)).astype(BF16)
    out[0] = 0.5 * dot(neumann[0], jnp.concatenate([here, there], axis=0))
    turned[0] = spread[0].T


def neumann_half(neumann, spread, residual, halo):
    subs, co, nb = spread.shape
    rhs = residual.shape[2]
    return pl.pallas_call(
        neumann_kernel,
        grid=(subs,),
        in_specs=[
            pl.BlockSpec((1, nb, nb), lambda s: (s, 0, 0)),
            pl.BlockSpec((1, co, nb), lambda s: (s, 0, 0)),
            whole(residual.shape),
            whole(halo.shape),
        ],
        out_specs=[
            pl.BlockSpec((1, nb, rhs), lambda s: (s, 0, 0)),
            pl.BlockSpec((1, nb, co), lambda s: (s, 0, 0)),
        ],
        out_shape=[
            jax.ShapeDtypeStruct((subs, nb, rhs), F32),
            jax.ShapeDtypeStruct((subs, nb, co), BF16),
        ],
        compiler_params=params(),
        cost_estimate=pl.CostEstimate(
            flops=2 * subs * nb * nb * rhs, bytes_accessed=4 * 10**6, transcendentals=0
        ),
        name="neumann_half",
    )(neumann, spread, residual, halo)


def coarse_kernel(other, turn, turned, ring, twin, part, out, near, far):
    s = pl.program_id(0)
    face = near.shape[0]
    at = turn[s]
    solved = jnp.where(other[s] == 1, twin[at].astype(F32), ring[at].astype(F32)).astype(BF16)
    found = part[0] + 0.5 * dot(turned[0], solved)
    out[0] = found

    @pl.when(s == 0)
    def _():
        near[...] = found[:face]

    @pl.when(s == pl.num_programs(0) - 1)
    def _():
        far[...] = found[face:]


def coarse_part(other, turn, turned, ring, twin, part):
    subs, nb, co = turned.shape
    rhs = ring.shape[2]
    return pl.pallas_call(
        coarse_kernel,
        grid=(subs,),
        in_specs=[
            smem(),
            smem(),
            pl.BlockSpec((1, nb, co), lambda s: (s, 0, 0)),
            whole(ring.shape),
            whole(twin.shape),
            pl.BlockSpec((1, nb, rhs), lambda s: (s, 0, 0)),
        ],
        out_specs=[
            pl.BlockSpec((1, nb, rhs), lambda s: (s, 0, 0)),
            whole((nb // 2, rhs)),
            whole((nb // 2, rhs)),
        ],
        out_shape=[
            jax.ShapeDtypeStruct((subs, nb, rhs), F32),
            jax.ShapeDtypeStruct((nb // 2, rhs), F32),
            jax.ShapeDtypeStruct((nb // 2, rhs), F32),
        ],
        compiler_params=params(),
        name="coarse_part",
    )(other, turn, turned, ring, twin, part)


def action(stiffness, coupling, interior, field):
    load = dot(coupling, field, TN).astype(BF16)
    inside = dot(interior, load).astype(BF16)
    return dot(stiffness, field) - dot(coupling, inside)


def operators(nb, ni, place):
    return [
        pl.BlockSpec((1, nb, nb), place),
        pl.BlockSpec((1, nb, ni), place),
        pl.BlockSpec((1, ni, ni), place),
    ]


def cost(steps, nb, ni, rhs):
    return pl.CostEstimate(
        flops=2 * steps * rhs * (nb * nb + 2 * nb * ni + ni * ni),
        bytes_accessed=2 * steps * (nb * nb + nb * ni + ni * ni),
        transcendentals=0,
    )


def act(stiffness, coupling, interior, own_p, far_p, own_d, far_d, own_r):
    face, rhs = own_p.shape
    field = jnp.concatenate(
        [jnp.concatenate([own_p, own_d], axis=1), jnp.concatenate([far_p, far_d], axis=1)], axis=0
    )
    both = action(stiffness[0], coupling[0], interior[0], field.astype(BF16))
    image, moved = both[:, :rhs], both[:, rhs:]
    parts = jnp.concatenate(
        [
            column_sum(own_r * own_p),
            column_sum(own_p * image[:face] + far_p * image[face:]),
            column_sum(own_p * moved[:face] + far_p * moved[face:])
            + column_sum(own_d * image[:face] + far_d * image[face:]),
            column_sum(own_d * moved[:face] + far_d * moved[face:]),
        ],
        axis=0,
    )
    return both, parts


def inner_kernel(stiffness, coupling, interior, pre, direction, residual, out, sums):
    i = pl.program_id(0)
    s = i + 1
    face = direction.shape[1]
    own_p = pre[s, :face] + pre[s - 1, face:]
    far_p = pre[s + 1, :face] + pre[s, face:]
    out[0], parts = act(
        stiffness, coupling, interior, own_p, far_p, direction[s], direction[s + 1], residual[s]
    )

    @pl.when(i == 0)
    def _():
        sums[...] = parts

    @pl.when(i > 0)
    def _():
        sums[...] += parts


def outer_kernel(
    stiffness,
    coupling,
    interior,
    pre,
    from_prev,
    from_next,
    direction,
    direction_halo,
    residual,
    earlier,
    out,
    copies,
    far,
    sums,
):
    i = pl.program_id(0)
    last = direction.shape[0] - 1
    s = i * last
    near = jnp.minimum(s + 1, last)
    behind = jnp.maximum(s - 1, 0)
    face = direction.shape[1]
    own_p = pre[s, :face] + jnp.where(i == 0, from_prev[...], pre[behind, face:])
    far_p = pre[s, face:] + jnp.where(i == 0, pre[near, :face], from_next[...])
    far_d = jnp.where(i == 0, direction[near], direction_halo[...])
    both, parts = act(
        stiffness, coupling, interior, own_p, far_p, direction[s], far_d, residual[s]
    )
    out[0] = both

    @pl.when(i == 0)
    def _():
        sums[...] = earlier[...] + parts

    @pl.when(i > 0)
    def _():
        far[...] = both[face:]
        total = sums[...] + parts
        for k in range(copies.shape[0]):
            copies[k] = total


def search_inner(stiffness, coupling, interior, pre, direction, residual):
    subs, nb, ni = coupling.shape
    rhs = direction.shape[2]
    rest = (pre, direction, residual)
    return pl.pallas_call(
        inner_kernel,
        grid=(subs - 2,),
        in_specs=operators(nb, ni, lambda i: (i + 1, 0, 0)) + [whole(x.shape) for x in rest],
        out_specs=[pl.BlockSpec((1, nb, 2 * rhs), lambda i: (i, 0, 0)), whole((4, rhs))],
        out_shape=[
            jax.ShapeDtypeStruct((subs - 2, nb, 2 * rhs), F32),
            jax.ShapeDtypeStruct((4, rhs), F32),
        ],
        compiler_params=params(LARGE),
        cost_estimate=cost(subs - 2, nb, ni, 2 * rhs),
        name="search_inner",
    )(stiffness, coupling, interior, *rest)


def search_outer(devices, stiffness, coupling, interior, *rest):
    subs, nb, ni = coupling.shape
    rhs = rest[0].shape[2]
    return pl.pallas_call(
        outer_kernel,
        grid=(2,),
        in_specs=operators(nb, ni, lambda i: ((subs - 1) * i, 0, 0)) + [whole(x.shape) for x in rest],
        out_specs=[
            pl.BlockSpec((1, nb, 2 * rhs), lambda i: (i, 0, 0)),
            whole((devices, 4, rhs)),
            whole((nb // 2, 2 * rhs)),
        ],
        out_shape=[
            jax.ShapeDtypeStruct((2, nb, 2 * rhs), F32),
            jax.ShapeDtypeStruct((devices, 4, rhs), F32),
            jax.ShapeDtypeStruct((nb // 2, 2 * rhs), F32),
        ],
        scratch_shapes=[pltpu.VMEM((4, rhs), F32)],
        compiler_params=params(LARGE),
        cost_estimate=cost(2, nb, ni, 2 * rhs),
        name="search_outer",
    )(stiffness, coupling, interior, *rest)


def update_kernel(
    sums, last_inner, pre, from_prev, outer, inside, before, direction, residual, solution, new_sol, new_res
):
    total = jnp.sum(sums[...], axis=0)
    inner = total[0:1]
    beta = inner / last_inner[...]
    curvature = total[1:2] + beta * (total[2:3] + beta * total[3:4])
    step = inner / curvature
    subs, face, rhs = direction.shape
    last = subs - 1

    def part(s):
        return outer[0] if s == 0 else outer[1] if s == last else inside[s - 1]

    for s in range(subs):
        behind = from_prev[...] if s == 0 else pre[s - 1, face:]
        both = part(s)[:face] + (before[...] if s == 0 else part(s - 1)[face:])
        search = pre[s, :face] + behind + beta * direction[s]
        image = both[:, :rhs] + beta * both[:, rhs:]
        new_sol[s] = solution[s] + step * search
        new_res[s] = residual[s] - step * image


def update(*args):
    shape = jax.ShapeDtypeStruct(args[-1].shape, F32)
    return pl.pallas_call(
        update_kernel, out_shape=[shape, shape], compiler_params=params(), name="update"
    )(*args)


def local(
    solution,
    residual,
    direction,
    last_inner,
    stiffness,
    coupling,
    interior,
    neumann,
    basis,
    panels,
    base_coarse,
    owners,
    prim_map,
    changed,
):
    groups = lax.axis_size("z")
    pieces = lax.axis_size("narrow")
    devices = groups * 2 * pieces
    face, rhs = residual.shape[1:]
    forward = [(i, (i + 1) % pieces) for i in range(pieces)]
    back = [((i + 1) % pieces, i) for i in range(pieces)]
    own = owners[:, 0]
    core = lax.axis_index("core")
    core_ref = core.astype(jnp.int32).reshape(1)

    halo = lax.ppermute(residual[0].astype(BF16), "narrow", back)
    direction_halo = lax.ppermute(direction[0], "narrow", back)
    other = ((own & 1) != core).astype(jnp.int32)
    turn = ((lax.axis_index("z") - (own >> 1)) % groups).astype(jnp.int32)
    keep, send, spread = place_panels(
        own, changed, core_ref, prim_map[:, None, :], jnp.swapaxes(basis, 1, 2), panels, residual, groups
    )
    keep, send = add_halo(own, core_ref, spread, halo, keep, send)
    mine = keep + lax.ppermute(send, "core", [(0, 1), (1, 0)])
    rows = mine.shape[1] // pieces
    mine, direction_halo, other, turn = lax.optimization_barrier((mine, direction_halo, other, turn))
    parts = lax.all_to_all(
        mine.reshape(groups * pieces, rows, rhs), ("z", "narrow"), 0, 0, tiled=True
    )
    copies = sum_copies(parts, pieces)
    packed = lax.all_to_all(copies, "narrow", 0, 0, tiled=True)
    solved = solve_block(packed.reshape(pieces * rows, rhs), base_coarse)

    turns = [lax.ppermute(solved, "z", [(i, (i + d) % groups) for i in range(groups)]) for d in range(1, groups)]
    ring = jnp.stack([solved] + turns)
    twin = lax.ppermute(ring, "core", [(0, 1), (1, 0)])
    given, spread, _ = lax.optimization_barrier((residual, spread, solved))
    part, turned = neumann_half(neumann, spread, given, halo)
    pre, near, far = coarse_part(other, turn, turned, ring, twin, part)
    from_prev = lax.ppermute(far, "narrow", forward)
    from_next = lax.ppermute(near, "narrow", back)
    inside, sums = search_inner(stiffness, coupling, interior, pre, direction, residual)
    outer, sums, behind = search_outer(
        devices,
        stiffness,
        coupling,
        interior,
        pre,
        from_prev,
        from_next,
        direction,
        direction_halo,
        residual,
        sums,
    )
    before = lax.ppermute(behind, "narrow", forward)
    sums = lax.all_to_all(sums, ("z", "core", "narrow"), 0, 0, tiled=True)
    return tuple(
        update(
            sums,
            last_inner[None],
            pre,
            from_prev,
            outer,
            inside,
            before,
            direction,
            residual,
            solution,
        )
    )


def solution(mesh):
    wide, narrow = mesh.devices.shape
    finer = Mesh(mesh.devices.reshape(wide // 2, 2, narrow), ("z", "core", "narrow"))
    split = ("z", "core", "narrow")
    in_specs = (
        P(split, None, None),
        P(split, None, None),
        P(split, None, None),
        P(),
        P(split, None, None),
        P(split, None, None),
        P(split, None, None),
        P(split, None, None),
        P(split, None, None),
        P(split, None, None),
        P(("z", "core"), None, None),
        P(split, None),
        P(split, None),
        P(split),
    )
    out_specs = (P(split, None, None), P(split, None, None))
    return jax.shard_map(local, mesh=finer, in_specs=in_specs, out_specs=out_specs, check_vma=False)
```

```python
import jax
import jax.numpy as jnp
from jax import lax
from jax.experimental import pallas as pl
from jax.experimental.pallas import tpu as pltpu
from jax.sharding import Mesh, PartitionSpec as P

F32 = jnp.float32
BF16 = jnp.bfloat16
NN = (((1,), (0,)), ((), ()))
NT = (((1,), (1,)), ((), ()))
TN = (((0,), (0,)), ((), ()))
SMALL = 16 * 1024 * 1024
LARGE = 24 * 1024 * 1024
INNER = 24 * 1024 * 1024
PLACE = 16 * 1024 * 1024
HIGHEST = lax.Precision.HIGHEST


def dot(a, b, dims=NN, precision=None):
    return lax.dot_general(a, b, dims, precision=precision, preferred_element_type=F32)


def smem():
    return pl.BlockSpec(memory_space=pltpu.SMEM)


def whole(shape):
    return pl.BlockSpec(shape, lambda *_: (0,) * len(shape))


def params(limit=SMALL):
    return pltpu.CompilerParams(vmem_limit_bytes=limit)


def stay(*arrays):
    return tuple(pltpu.with_memory_space_constraint(x, pltpu.HBM) for x in arrays)


def column_sum(value):
    return jnp.sum(value, axis=0, keepdims=True)


def chosen(pm, s, co):
    rows = lax.broadcasted_iota(jnp.int32, (co, pm.shape[1]), 0)
    return (rows == pm[pl.ds(s, 1)]).astype(F32).astype(BF16)


def place_kernel(own, chg, core, pm, basis, panel, res, keep, send, edge, held, sems):
    s = pl.program_id(0)
    last = pl.num_programs(0) - 1
    co = edge.shape[0]
    half = co // 2
    face = res.shape[1]

    @pl.when(s == 0)
    def _():
        held[...] = jnp.zeros_like(held)

    select = chosen(pm, s, co)
    wide_basis = dot(select, basis[0]).astype(BF16)
    placed = dot(dot(select, panel[0]).astype(BF16), select, NT) * chg[s].astype(F32)
    here = res[s].astype(BF16)
    there = res[jnp.minimum(s + 1, last)].astype(BF16)
    rhs = dot(wide_basis[:, :face], here)
    rhs += jnp.where(s < last, dot(wide_basis[:, face:], there), 0.0)
    owner = own[s]
    place = owner >> 1
    leaves = (owner & 1) ^ core[0]
    held[leaves, place, 0:half] += placed[:half, :half]
    held[leaves, place, half:co] += placed[half:, :half]
    held[leaves, place, co : co + half] += placed[half:, half:]
    held[leaves, place, co + half :] += rhs

    @pl.when(s == last)
    def _():
        edge[...] = wide_basis[:, face:]
        first = pltpu.make_async_copy(held.at[1], send, sems.at[0])
        second = pltpu.make_async_copy(held.at[0], keep, sems.at[1])
        first.start()
        second.start()
        first.wait()
        second.wait()


def place_panels(own, chg, core, prim_map, basis, panels, residual, groups):
    subs, npr, nb = basis.shape
    co = 2 * residual.shape[2]
    rows = 3 * (co // 2) + co
    packed = (groups, rows, co // 2)
    hbm = pl.BlockSpec(memory_space=pl.ANY)
    return pl.pallas_call(
        place_kernel,
        grid=(subs,),
        in_specs=[
            smem(),
            smem(),
            smem(),
            whole((subs, npr)),
            pl.BlockSpec((1, npr, nb), lambda s: (s, 0, 0)),
            pl.BlockSpec((1, npr, npr), lambda s: (s, 0, 0)),
            whole(residual.shape),
        ],
        out_specs=[hbm, hbm, whole((co, nb // 2))],
        out_shape=[
            jax.ShapeDtypeStruct(packed, F32),
            jax.ShapeDtypeStruct(packed, F32),
            jax.ShapeDtypeStruct((co, nb // 2), BF16),
        ],
        scratch_shapes=[pltpu.VMEM((2,) + packed, F32), pltpu.SemaphoreType.DMA((2,))],
        compiler_params=params(PLACE),
        cost_estimate=pl.CostEstimate(flops=10**9, bytes_accessed=6 * 10**6, transcendentals=0),
        name="place_panels",
    )(*stay(own, chg), core, *stay(prim_map, basis, panels, residual))


def halo_kernel(own, core, edge, halo, keep_in, send_in, keep, send, held, sem):
    del keep_in, send_in
    owner = own[own.shape[0] - 1]
    place = owner >> 1
    other = (owner & 1) != core[0]
    rows = held.shape[0]

    def add(to):
        part = to.at[place, pl.ds(to.shape[1] - rows, rows)]
        fetch = pltpu.make_async_copy(part, held, sem)
        fetch.start()
        value = dot(edge[...], halo[...])
        fetch.wait()
        held[...] += value
        put = pltpu.make_async_copy(held, part, sem)
        put.start()
        put.wait()

    @pl.when(other)
    def _():
        add(send)

    @pl.when(jnp.logical_not(other))
    def _():
        add(keep)


def add_halo(own, core, edge, halo, keep, send):
    hbm = pl.BlockSpec(memory_space=pl.ANY)
    return pl.pallas_call(
        halo_kernel,
        grid=(1,),
        in_specs=[
            smem(),
            smem(),
            whole(edge.shape),
            whole(halo.shape),
            hbm,
            hbm,
        ],
        out_specs=[hbm, hbm],
        out_shape=[jax.ShapeDtypeStruct(keep.shape, F32), jax.ShapeDtypeStruct(send.shape, F32)],
        input_output_aliases={4: 0, 5: 1},
        scratch_shapes=[pltpu.VMEM((edge.shape[0], halo.shape[1]), F32), pltpu.SemaphoreType.DMA],
        compiler_params=params(PLACE),
        name="add_halo",
    )(own, core, edge, halo, keep, send)


def gather_kernel(parts, out):
    total = jnp.sum(parts[...], axis=0)
    for i in range(out.shape[0]):
        out[i] = total


def sum_copies(parts, copies):
    return pl.pallas_call(
        gather_kernel,
        out_shape=jax.ShapeDtypeStruct((copies,) + parts.shape[1:], F32),
        compiler_params=params(),
        name="sum_copies",
    )(parts)


MOST_STEPS = 24


def inverse(matrix):
    n = matrix.shape[0]
    lanes = lax.broadcasted_iota(jnp.int32, (8, n), 1)
    subl = lax.broadcasted_iota(jnp.int32, (8, n), 0)
    tiles = tuple(matrix[8 * i : 8 * i + 8] for i in range(n // 8))

    def group(_, tiles):
        tiles = list(tiles)
        for j in range(8):
            pivot_row = tiles[0][j : j + 1, :]
            scale = 1.0 / pivot_row[:, j : j + 1]
            row = jnp.where(lanes[:1] == j, scale, pivot_row * scale)
            for i, tile in enumerate(tiles):
                new = jnp.where(lanes == j, 0.0, tile) - tile[:, j : j + 1] * row
                if i == 0:
                    new = jnp.where(subl == j, row, new)
                tiles[i] = new
        return tuple(pltpu.roll(tile, n - 8, 1) for tile in tiles[1:] + tiles[:1])

    return jnp.concatenate(lax.fori_loop(0, n // 8, group, tiles), axis=0)


def split(value, terms):
    found = []
    for _ in range(terms):
        found.append(value.astype(BF16))
        value = value - found[-1].astype(F32)
    return found


def eliminate(matrix, right):
    half = matrix.shape[0] // 2
    a21 = matrix[half:, :half]
    b1, b2 = right[:half], right[half:]
    inv1 = inverse(matrix[:half, :half])
    carry = dot(a21, inv1, NN, HIGHEST)
    inv2 = inverse(matrix[half:, half:] - dot(carry, a21, NT, HIGHEST))
    x2 = dot(inv2, b2 - dot(carry, b1, NN, HIGHEST), NN, HIGHEST)
    x1 = dot(inv1, b1, NN, HIGHEST) - dot(carry, x2, TN, HIGHEST)
    return x1, x2


def solve_kernel(packed, base, out, mat, terms, x, r, p):
    co = out.shape[0]
    half = co // 2
    a21 = packed[half:co]
    mat[:half, :half] = packed[:half] + base[0, :half, :half]
    mat[half:, :half] = a21 + base[0, half:, :half]
    mat[:half, half:] = a21.T + base[0, :half, half:]
    mat[half:, half:] = packed[co : co + half] + base[0, half:, half:]
    rows = lax.broadcasted_iota(jnp.int32, (co, co), 0)
    columns = lax.broadcasted_iota(jnp.int32, (co, co), 1)
    scale = 1.0 / jnp.sum(jnp.where(rows == columns, mat[...], 0.0), axis=1, keepdims=True)
    for i, term in enumerate(split(mat[...], 3)):
        terms[i] = term
    right = packed[co + half :]
    size = jnp.max(jnp.abs(right), axis=0, keepdims=True)
    size = jnp.where(size > 0.0, size, 1.0)
    right = right * (1.0 / size)

    def times(value):
        n = value.shape[1]
        v1, v2, v3 = split(value, 3)
        pair = jnp.concatenate([v1, v2], axis=1)
        first = dot(terms[0], pair)
        second = dot(terms[1], pair)
        small = second[:, n:] + dot(terms[0], v3) + dot(terms[2], v1)
        return first[:, :n] + (first[:, n:] + second[:, :n] + small)

    x[...] = jnp.zeros_like(right)
    r[...] = right
    p[...] = scale * right
    start = column_sum(right * (scale * right))

    def steps(state):
        count, norm, _ = state
        for _ in range(2):
            image = times(p[...])
            energy = column_sum(p[...] * image)
            length = jnp.where(energy > 0.0, norm / energy, 0.0)
            x[...] += length * p[...]
            left = r[...] - length * image
            r[...] = left
            scaled = scale * left
            new = column_sum(left * scaled)
            p[...] = scaled + jnp.where(norm > 0.0, new / norm, 0.0) * p[...]
            norm = new
        return count + 2, norm, jnp.max(norm - 1e-13 * start) > 0.0

    lax.while_loop(
        lambda state: state[2] & (state[0] < MOST_STEPS), steps, (jnp.int32(0), start, jnp.bool_(True))
    )
    left = right - dot(mat[...], x[...], NN, HIGHEST)
    solved = jnp.max(column_sum(left * (scale * left)) - 1e-11 * start) <= 0.0

    @pl.when(solved)
    def _():
        out[...] = (x[...] * size).astype(BF16)

    @pl.when(jnp.logical_not(solved))
    def _():
        x1, x2 = eliminate(mat[...], packed[co + half :])
        out[:half] = x1.astype(BF16)
        out[half:] = x2.astype(BF16)


def solve_block(packed, base):
    co = base.shape[1]
    rhs = packed.shape[1]
    return pl.pallas_call(
        solve_kernel,
        out_shape=jax.ShapeDtypeStruct((co, rhs), BF16),
        scratch_shapes=[
            pltpu.VMEM((co, co), F32),
            pltpu.VMEM((3, co, co), BF16),
            pltpu.VMEM((co, rhs), F32),
            pltpu.VMEM((co, rhs), F32),
            pltpu.VMEM((co, rhs), F32),
        ],
        compiler_params=params(),
        name="solve_block",
    )(packed, base)


def neumann_kernel(pm, neumann, basis, res, halo, out, turned):
    s = pl.program_id(0)
    last = pl.num_programs(0) - 1
    here = res[s].astype(BF16)
    there = jnp.where(s < last, res[jnp.minimum(s + 1, last)], halo[...].astype(F32)).astype(BF16)
    out[0] = 0.5 * dot(neumann[0], jnp.concatenate([here, there], axis=0))
    turned[0] = dot(chosen(pm, s, turned.shape[2]), basis[0]).astype(BF16).T


def neumann_half(prim_map, neumann, basis, residual, halo):
    subs, npr, nb = basis.shape
    rhs = residual.shape[2]
    co = 2 * rhs
    return pl.pallas_call(
        neumann_kernel,
        grid=(subs,),
        in_specs=[
            whole((subs, npr)),
            pl.BlockSpec((1, nb, nb), lambda s: (s, 0, 0)),
            pl.BlockSpec((1, npr, nb), lambda s: (s, 0, 0)),
            whole(residual.shape),
            whole(halo.shape),
        ],
        out_specs=[
            pl.BlockSpec((1, nb, rhs), lambda s: (s, 0, 0)),
            pl.BlockSpec((1, nb, co), lambda s: (s, 0, 0)),
        ],
        out_shape=[
            jax.ShapeDtypeStruct((subs, nb, rhs), F32),
            jax.ShapeDtypeStruct((subs, nb, co), BF16),
        ],
        compiler_params=params(),
        cost_estimate=pl.CostEstimate(
            flops=2 * subs * nb * nb * rhs, bytes_accessed=4 * 10**6, transcendentals=0
        ),
        name="neumann_half",
    )(*stay(prim_map, neumann, basis), residual, halo)


def coarse_kernel(own, core, z, turned, ring, twin, part, out, near, far):
    s = pl.program_id(0)
    face = far.shape[0]
    groups = ring.shape[0]
    at = lax.rem(z[0] - (own[s] >> 1) + groups, groups)
    solved = jnp.where((own[s] & 1) != core[0], twin[at].astype(F32), ring[at].astype(F32)).astype(BF16)
    found = part[0] + 0.5 * dot(turned[0], solved)
    out[0] = found

    @pl.when(s == 0)
    def _():
        near[...] = found[:face]

    @pl.when(s == pl.num_programs(0) - 1)
    def _():
        far[...] = found[face:]


def coarse_part(own, core, z, turned, ring, twin, part):
    subs, nb, co = turned.shape
    rhs = ring.shape[2]
    return pl.pallas_call(
        coarse_kernel,
        grid=(subs,),
        in_specs=[
            smem(),
            smem(),
            smem(),
            pl.BlockSpec((1, nb, co), lambda s: (s, 0, 0)),
            whole(ring.shape),
            whole(twin.shape),
            pl.BlockSpec((1, nb, rhs), lambda s: (s, 0, 0)),
        ],
        out_specs=[
            pl.BlockSpec((1, nb, rhs), lambda s: (s, 0, 0)),
            whole((nb // 2, rhs)),
            whole((nb // 2, rhs)),
        ],
        out_shape=[
            jax.ShapeDtypeStruct((subs, nb, rhs), F32),
            jax.ShapeDtypeStruct((nb // 2, rhs), F32),
            jax.ShapeDtypeStruct((nb // 2, rhs), F32),
        ],
        compiler_params=params(),
        name="coarse_part",
    )(own, core, z, turned, ring, twin, part)


def action(stiffness, coupling, interior, field):
    across = field.T.astype(BF16)
    load = dot(across, coupling).astype(BF16)
    inside = dot(load, interior, NT).astype(BF16)
    return dot(stiffness, field.astype(BF16)) - dot(coupling, inside, NT)


def operators(nb, ni, place):
    return [
        pl.BlockSpec((1, nb, nb), place),
        pl.BlockSpec((1, nb, ni), place),
        pl.BlockSpec((1, ni, ni), place),
    ]


def cost(steps, nb, ni, rhs):
    return pl.CostEstimate(
        flops=2 * steps * rhs * (nb * nb + 2 * nb * ni + ni * ni),
        bytes_accessed=2 * steps * (nb * nb + nb * ni + ni * ni),
        transcendentals=0,
    )


def act(stiffness, coupling, interior, own_p, far_p, own_d, far_d, own_r):
    face, rhs = own_p.shape
    field = jnp.concatenate(
        [jnp.concatenate([own_p, own_d], axis=1), jnp.concatenate([far_p, far_d], axis=1)], axis=0
    )
    both = action(stiffness[0], coupling[0], interior[0], field)
    image, moved = both[:, :rhs], both[:, rhs:]
    parts = jnp.concatenate(
        [
            column_sum(own_r * own_p),
            column_sum(own_p * image[:face] + far_p * image[face:]),
            column_sum(own_p * moved[:face] + far_p * moved[face:])
            + column_sum(own_d * image[:face] + far_d * image[face:]),
            column_sum(own_d * moved[:face] + far_d * moved[face:]),
        ],
        axis=0,
    )
    return both, parts


def inner_kernel(stiffness, coupling, interior, pre, direction, residual, out, sums):
    i = pl.program_id(0)
    s = i + 1
    face = direction.shape[1]
    own_p = pre[s, :face] + pre[s - 1, face:]
    far_p = pre[s + 1, :face] + pre[s, face:]
    out[0], parts = act(
        stiffness, coupling, interior, own_p, far_p, direction[s], direction[s + 1], residual[s]
    )

    @pl.when(i == 0)
    def _():
        sums[...] = parts

    @pl.when(i > 0)
    def _():
        sums[...] += parts


def outer_kernel(
    stiffness,
    coupling,
    interior,
    pre,
    from_prev,
    from_next,
    direction,
    direction_halo,
    residual,
    earlier,
    out,
    copies,
    far,
    sums,
):
    i = pl.program_id(0)
    last = direction.shape[0] - 1
    s = i * last
    near = jnp.minimum(s + 1, last)
    behind = jnp.maximum(s - 1, 0)
    face = direction.shape[1]
    own_p = pre[s, :face] + jnp.where(i == 0, from_prev[...], pre[behind, face:])
    far_p = pre[s, face:] + jnp.where(i == 0, pre[near, :face], from_next[...])
    far_d = jnp.where(i == 0, direction[near], direction_halo[...])
    both, parts = act(
        stiffness, coupling, interior, own_p, far_p, direction[s], far_d, residual[s]
    )
    out[0] = both

    @pl.when(i == 0)
    def _():
        sums[...] = earlier[...] + parts

    @pl.when(i > 0)
    def _():
        far[...] = both[face:]
        total = sums[...] + parts
        for k in range(copies.shape[0]):
            copies[k] = total


def search_inner(stiffness, coupling, interior, pre, direction, residual):
    subs, nb, ni = coupling.shape
    rhs = direction.shape[2]
    rest = (pre, direction, residual)
    return pl.pallas_call(
        inner_kernel,
        grid=(subs - 2,),
        in_specs=operators(nb, ni, lambda i: (i + 1, 0, 0)) + [whole(x.shape) for x in rest],
        out_specs=[pl.BlockSpec((1, nb, 2 * rhs), lambda i: (i, 0, 0)), whole((4, rhs))],
        out_shape=[
            jax.ShapeDtypeStruct((subs - 2, nb, 2 * rhs), F32),
            jax.ShapeDtypeStruct((4, rhs), F32),
        ],
        compiler_params=params(INNER),
        cost_estimate=cost(subs - 2, nb, ni, 2 * rhs),
        name="search_inner",
    )(*stay(stiffness, coupling, interior), *rest)


def search_outer(devices, stiffness, coupling, interior, *rest):
    subs, nb, ni = coupling.shape
    rhs = rest[0].shape[2]
    return pl.pallas_call(
        outer_kernel,
        grid=(2,),
        in_specs=operators(nb, ni, lambda i: ((subs - 1) * i, 0, 0)) + [whole(x.shape) for x in rest],
        out_specs=[
            pl.BlockSpec((1, nb, 2 * rhs), lambda i: (i, 0, 0)),
            whole((devices, 4, rhs)),
            whole((nb // 2, 2 * rhs)),
        ],
        out_shape=[
            jax.ShapeDtypeStruct((2, nb, 2 * rhs), F32),
            jax.ShapeDtypeStruct((devices, 4, rhs), F32),
            jax.ShapeDtypeStruct((nb // 2, 2 * rhs), F32),
        ],
        scratch_shapes=[pltpu.VMEM((4, rhs), F32)],
        compiler_params=params(LARGE),
        cost_estimate=cost(2, nb, ni, 2 * rhs),
        name="search_outer",
    )(*stay(stiffness, coupling, interior), *rest)


def update_kernel(
    sums, last_inner, pre, from_prev, outer, inside, before, direction, residual, solution, new_sol, new_res
):
    total = jnp.sum(sums[...], axis=0)
    inner = total[0:1]
    beta = inner / last_inner[...]
    curvature = total[1:2] + beta * (total[2:3] + beta * total[3:4])
    step = inner / curvature
    subs, face, rhs = direction.shape
    last = subs - 1

    def part(s):
        return outer[0] if s == 0 else outer[1] if s == last else inside[s - 1]

    for s in range(subs):
        behind = from_prev[...] if s == 0 else pre[s - 1, face:]
        both = part(s)[:face] + (before[...] if s == 0 else part(s - 1)[face:])
        search = pre[s, :face] + behind + beta * direction[s]
        image = both[:, :rhs] + beta * both[:, rhs:]
        new_sol[s] = solution[s] + step * search
        new_res[s] = residual[s] - step * image


def update(*args):
    shape = jax.ShapeDtypeStruct(args[-1].shape, F32)
    return pl.pallas_call(
        update_kernel, out_shape=[shape, shape], compiler_params=params(), name="update"
    )(*args)


def local(
    solution,
    residual,
    direction,
    last_inner,
    stiffness,
    coupling,
    interior,
    neumann,
    basis,
    panels,
    base_coarse,
    owners,
    prim_map,
    changed,
):
    groups = lax.axis_size("z")
    pieces = lax.axis_size("narrow")
    devices = groups * 2 * pieces
    face, rhs = residual.shape[1:]
    forward = [(i, (i + 1) % pieces) for i in range(pieces)]
    back = [((i + 1) % pieces, i) for i in range(pieces)]
    own = owners[:, 0]
    core = lax.axis_index("core")
    core_ref = core.astype(jnp.int32).reshape(1)
    z_ref = lax.axis_index("z").astype(jnp.int32).reshape(1)

    halo = lax.ppermute(residual[0].astype(BF16), "narrow", back)
    basis = jnp.swapaxes(basis, 1, 2)
    keep, send, edge = place_panels(own, changed, core_ref, prim_map, basis, panels, residual, groups)
    keep, send = add_halo(own, core_ref, edge, halo, keep, send)
    mine = keep + lax.ppermute(send, "core", [(0, 1), (1, 0)])
    rows = mine.shape[1] // pieces
    parts = lax.all_to_all(
        mine.reshape(groups * pieces, rows, rhs), ("z", "narrow"), 0, 0, tiled=True
    )
    copies = sum_copies(parts, pieces)
    packed = lax.all_to_all(copies, "narrow", 0, 0, tiled=True)
    solved = solve_block(packed.reshape(pieces * rows, rhs), base_coarse)

    turns = [lax.ppermute(solved, "z", [(i, (i + d) % groups) for i in range(groups)]) for d in range(1, groups)]
    given, heading, _ = lax.optimization_barrier((residual, direction[0], solved))
    direction_halo = lax.ppermute(heading, "narrow", back)
    part, turned = neumann_half(prim_map, neumann, basis, given, halo)
    turns, part, turned = lax.optimization_barrier((turns, part, turned))
    ring = jnp.stack([solved] + turns)
    twin = lax.ppermute(ring, "core", [(0, 1), (1, 0)])
    pre, near, far = coarse_part(own, core_ref, z_ref, turned, ring, twin, part)
    from_prev = lax.ppermute(far, "narrow", forward)
    from_next = lax.ppermute(near, "narrow", back)
    inside, sums = search_inner(stiffness, coupling, interior, pre, direction, residual)
    outer, sums, behind = search_outer(
        devices,
        stiffness,
        coupling,
        interior,
        pre,
        from_prev,
        from_next,
        direction,
        direction_halo,
        residual,
        sums,
    )
    before = lax.ppermute(behind, "narrow", forward)
    sums = lax.all_to_all(sums, ("z", "core", "narrow"), 0, 0, tiled=True)
    return tuple(
        update(
            sums,
            last_inner[None],
            pre,
            from_prev,
            outer,
            inside,
            before,
            direction,
            residual,
            solution,
        )
    )


def solution(mesh):
    wide, narrow = mesh.devices.shape
    finer = Mesh(mesh.devices.reshape(wide // 2, 2, narrow), ("z", "core", "narrow"))
    split = ("z", "core", "narrow")
    in_specs = (
        P(split, None, None),
        P(split, None, None),
        P(split, None, None),
        P(),
        P(split, None, None),
        P(split, None, None),
        P(split, None, None),
        P(split, None, None),
        P(split, None, None),
        P(split, None, None),
        P(("z", "core"), None, None),
        P(split, None),
        P(split, None),
        P(split),
    )
    out_specs = (P(split, None, None), P(split, None, None))
    return jax.shard_map(local, mesh=finer, in_specs=in_specs, out_specs=out_specs, check_vma=False)
```

```python
import jax
import jax.numpy as jnp
from jax import lax
from jax.experimental import pallas as pl
from jax.experimental.pallas import tpu as pltpu
from jax.sharding import Mesh, PartitionSpec as P

F32 = jnp.float32
BF16 = jnp.bfloat16
NN = (((1,), (0,)), ((), ()))
NT = (((1,), (1,)), ((), ()))
TN = (((0,), (0,)), ((), ()))
SMALL = 16 * 1024 * 1024
LARGE = 24 * 1024 * 1024
PLACE = 16 * 1024 * 1024
HIGHEST = lax.Precision.HIGHEST


def dot(a, b, dims=NN, precision=None):
    return lax.dot_general(a, b, dims, precision=precision, preferred_element_type=F32)


def smem():
    return pl.BlockSpec(memory_space=pltpu.SMEM)


def whole(shape):
    return pl.BlockSpec(shape, lambda *_: (0,) * len(shape))


def params(limit=SMALL):
    return pltpu.CompilerParams(vmem_limit_bytes=limit)


def stay(*arrays):
    return tuple(pltpu.with_memory_space_constraint(x, pltpu.HBM) for x in arrays)


def column_sum(value):
    return jnp.sum(value, axis=0, keepdims=True)


def chosen(pm, s, co):
    rows = lax.broadcasted_iota(jnp.int32, (co, pm.shape[1]), 0)
    return (rows == pm[pl.ds(s, 1)]).astype(F32).astype(BF16)


def place_kernel(own, chg, core, pm, basis, panel, res, keep, send, edge, held, sems):
    s = pl.program_id(0)
    last = pl.num_programs(0) - 1
    co = edge.shape[0]
    half = co // 2
    face = res.shape[1]

    @pl.when(s == 0)
    def _():
        held[...] = jnp.zeros_like(held)

    select = chosen(pm, s, co)
    wide_basis = dot(select, basis[0]).astype(BF16)
    placed = dot(dot(select, panel[0]).astype(BF16), select, NT) * chg[s].astype(F32)
    here = res[s].astype(BF16)
    there = res[jnp.minimum(s + 1, last)].astype(BF16)
    rhs = dot(wide_basis[:, :face], here)
    rhs += jnp.where(s < last, dot(wide_basis[:, face:], there), 0.0)
    owner = own[s]
    place = owner >> 1
    leaves = (owner & 1) ^ core[0]
    held[leaves, place, 0:half] += placed[:half, :half]
    held[leaves, place, half:co] += placed[half:, :half]
    held[leaves, place, co : co + half] += placed[half:, half:]
    held[leaves, place, co + half :] += rhs

    @pl.when(s == last)
    def _():
        edge[...] = wide_basis[:, face:]
        first = pltpu.make_async_copy(held.at[1], send, sems.at[0])
        second = pltpu.make_async_copy(held.at[0], keep, sems.at[1])
        first.start()
        second.start()
        first.wait()
        second.wait()


def place_panels(own, chg, core, prim_map, basis, panels, residual, groups):
    subs, npr, nb = basis.shape
    co = 2 * residual.shape[2]
    rows = 3 * (co // 2) + co
    packed = (groups, rows, co // 2)
    hbm = pl.BlockSpec(memory_space=pl.ANY)
    return pl.pallas_call(
        place_kernel,
        grid=(subs,),
        in_specs=[
            smem(),
            smem(),
            smem(),
            whole((subs, npr)),
            pl.BlockSpec((1, npr, nb), lambda s: (s, 0, 0)),
            pl.BlockSpec((1, npr, npr), lambda s: (s, 0, 0)),
            whole(residual.shape),
        ],
        out_specs=[hbm, hbm, whole((co, nb // 2))],
        out_shape=[
            jax.ShapeDtypeStruct(packed, F32),
            jax.ShapeDtypeStruct(packed, F32),
            jax.ShapeDtypeStruct((co, nb // 2), BF16),
        ],
        scratch_shapes=[pltpu.VMEM((2,) + packed, F32), pltpu.SemaphoreType.DMA((2,))],
        compiler_params=params(PLACE),
        cost_estimate=pl.CostEstimate(flops=10**9, bytes_accessed=6 * 10**6, transcendentals=0),
        name="place_panels",
    )(*stay(own, chg), core, *stay(prim_map, basis, panels, residual))


def halo_kernel(own, core, edge, halo, keep_in, send_in, keep, send, held, sem):
    del keep_in, send_in
    owner = own[own.shape[0] - 1]
    place = owner >> 1
    other = (owner & 1) != core[0]
    rows = held.shape[0]

    def add(to):
        part = to.at[place, pl.ds(to.shape[1] - rows, rows)]
        fetch = pltpu.make_async_copy(part, held, sem)
        fetch.start()
        value = dot(edge[...], halo[...])
        fetch.wait()
        held[...] += value
        put = pltpu.make_async_copy(held, part, sem)
        put.start()
        put.wait()

    @pl.when(other)
    def _():
        add(send)

    @pl.when(jnp.logical_not(other))
    def _():
        add(keep)


def add_halo(own, core, edge, halo, keep, send):
    hbm = pl.BlockSpec(memory_space=pl.ANY)
    return pl.pallas_call(
        halo_kernel,
        grid=(1,),
        in_specs=[
            smem(),
            smem(),
            whole(edge.shape),
            whole(halo.shape),
            hbm,
            hbm,
        ],
        out_specs=[hbm, hbm],
        out_shape=[jax.ShapeDtypeStruct(keep.shape, F32), jax.ShapeDtypeStruct(send.shape, F32)],
        input_output_aliases={4: 0, 5: 1},
        scratch_shapes=[pltpu.VMEM((edge.shape[0], halo.shape[1]), F32), pltpu.SemaphoreType.DMA],
        compiler_params=params(PLACE),
        name="add_halo",
    )(own, core, edge, halo, keep, send)


def gather_kernel(parts, out):
    total = jnp.sum(parts[...], axis=0)
    for i in range(out.shape[0]):
        out[i] = total


def sum_copies(parts, copies):
    return pl.pallas_call(
        gather_kernel,
        out_shape=jax.ShapeDtypeStruct((copies,) + parts.shape[1:], F32),
        compiler_params=params(),
        name="sum_copies",
    )(parts)


MOST_STEPS = 24


def inverse(matrix):
    n = matrix.shape[0]
    lanes = lax.broadcasted_iota(jnp.int32, (8, n), 1)
    subl = lax.broadcasted_iota(jnp.int32, (8, n), 0)
    tiles = tuple(matrix[8 * i : 8 * i + 8] for i in range(n // 8))

    def group(_, tiles):
        tiles = list(tiles)
        for j in range(8):
            pivot_row = tiles[0][j : j + 1, :]
            scale = 1.0 / pivot_row[:, j : j + 1]
            row = jnp.where(lanes[:1] == j, scale, pivot_row * scale)
            for i, tile in enumerate(tiles):
                new = jnp.where(lanes == j, 0.0, tile) - tile[:, j : j + 1] * row
                if i == 0:
                    new = jnp.where(subl == j, row, new)
                tiles[i] = new
        return tuple(pltpu.roll(tile, n - 8, 1) for tile in tiles[1:] + tiles[:1])

    return jnp.concatenate(lax.fori_loop(0, n // 8, group, tiles), axis=0)


def split(value, terms):
    found = []
    for _ in range(terms):
        found.append(value.astype(BF16))
        value = value - found[-1].astype(F32)
    return found


def eliminate(matrix, right):
    half = matrix.shape[0] // 2
    a21 = matrix[half:, :half]
    b1, b2 = right[:half], right[half:]
    inv1 = inverse(matrix[:half, :half])
    carry = dot(a21, inv1, NN, HIGHEST)
    inv2 = inverse(matrix[half:, half:] - dot(carry, a21, NT, HIGHEST))
    x2 = dot(inv2, b2 - dot(carry, b1, NN, HIGHEST), NN, HIGHEST)
    x1 = dot(inv1, b1, NN, HIGHEST) - dot(carry, x2, TN, HIGHEST)
    return x1, x2


def solve_kernel(packed, base, out, mat, terms, x, r, p):
    co = out.shape[0]
    half = co // 2
    a21 = packed[half:co]
    mat[:half, :half] = packed[:half] + base[0, :half, :half]
    mat[half:, :half] = a21 + base[0, half:, :half]
    mat[:half, half:] = a21.T + base[0, :half, half:]
    mat[half:, half:] = packed[co : co + half] + base[0, half:, half:]
    rows = lax.broadcasted_iota(jnp.int32, (co, co), 0)
    columns = lax.broadcasted_iota(jnp.int32, (co, co), 1)
    scale = 1.0 / jnp.sum(jnp.where(rows == columns, mat[...], 0.0), axis=1, keepdims=True)
    for i, term in enumerate(split(mat[...], 3)):
        terms[i] = term
    right = packed[co + half :]
    size = jnp.max(jnp.abs(right), axis=0, keepdims=True)
    size = jnp.where(size > 0.0, size, 1.0)
    right = right * (1.0 / size)

    def times(value):
        n = value.shape[1]
        v1, v2, v3 = split(value, 3)
        pair = jnp.concatenate([v1, v2], axis=1)
        first = dot(terms[0], pair)
        second = dot(terms[1], pair)
        small = second[:, n:] + dot(terms[0], v3) + dot(terms[2], v1)
        return first[:, :n] + (first[:, n:] + second[:, :n] + small)

    x[...] = jnp.zeros_like(right)
    r[...] = right
    p[...] = scale * right
    start = column_sum(right * (scale * right))

    def steps(state):
        count, norm, _ = state
        for _ in range(2):
            image = times(p[...])
            energy = column_sum(p[...] * image)
            length = jnp.where(energy > 0.0, norm / energy, 0.0)
            x[...] += length * p[...]
            left = r[...] - length * image
            r[...] = left
            scaled = scale * left
            new = column_sum(left * scaled)
            p[...] = scaled + jnp.where(norm > 0.0, new / norm, 0.0) * p[...]
            norm = new
        return count + 2, norm, jnp.max(norm - 1e-12 * start) > 0.0

    lax.while_loop(
        lambda state: state[2] & (state[0] < MOST_STEPS), steps, (jnp.int32(0), start, jnp.bool_(True))
    )
    left = right - dot(mat[...], x[...], NN, HIGHEST)
    solved = jnp.max(column_sum(left * (scale * left)) - 1e-11 * start) <= 0.0

    @pl.when(solved)
    def _():
        out[...] = (x[...] * size).astype(BF16)

    @pl.when(jnp.logical_not(solved))
    def _():
        x1, x2 = eliminate(mat[...], packed[co + half :])
        out[:half] = x1.astype(BF16)
        out[half:] = x2.astype(BF16)


def solve_block(packed, base):
    co = base.shape[1]
    rhs = packed.shape[1]
    return pl.pallas_call(
        solve_kernel,
        out_shape=jax.ShapeDtypeStruct((co, rhs), BF16),
        scratch_shapes=[
            pltpu.VMEM((co, co), F32),
            pltpu.VMEM((3, co, co), BF16),
            pltpu.VMEM((co, rhs), F32),
            pltpu.VMEM((co, rhs), F32),
            pltpu.VMEM((co, rhs), F32),
        ],
        compiler_params=params(),
        name="solve_block",
    )(packed, base)


def fetches(subs, sources, places, sems):
    return [
        pltpu.make_async_copy(source.at[s], place.at[j], sems.at[k, j])
        for k, (source, place) in enumerate(zip(sources, places))
        for j, s in enumerate(subs)
    ]


def fetched(operators):
    return [jax.ShapeDtypeStruct((2,) + x.shape[1:], x.dtype) for x in operators]


ANYWHERE = pl.BlockSpec(memory_space=pl.ANY)
IN_HBM = pl.BlockSpec(memory_space=pltpu.HBM)


def neumann_kernel(pm, neumann, basis, res, halo, out, turned):
    s = pl.program_id(0)
    last = pl.num_programs(0) - 1
    here = res[s].astype(BF16)
    there = jnp.where(s < last, res[jnp.minimum(s + 1, last)], halo[...].astype(F32)).astype(BF16)
    out[0] = 0.5 * dot(neumann[0], jnp.concatenate([here, there], axis=0))
    turned[0] = dot(chosen(pm, s, turned.shape[2]), basis[0]).astype(BF16).T


def neumann_half(prim_map, neumann, basis, residual, halo):
    subs, npr, nb = basis.shape
    rhs = residual.shape[2]
    co = 2 * rhs
    return pl.pallas_call(
        neumann_kernel,
        grid=(subs,),
        in_specs=[
            whole((subs, npr)),
            pl.BlockSpec((1, nb, nb), lambda s: (s, 0, 0)),
            pl.BlockSpec((1, npr, nb), lambda s: (s, 0, 0)),
            whole(residual.shape),
            whole(halo.shape),
        ],
        out_specs=[
            pl.BlockSpec((1, nb, rhs), lambda s: (s, 0, 0)),
            pl.BlockSpec((1, nb, co), lambda s: (s, 0, 0)),
        ],
        out_shape=[
            jax.ShapeDtypeStruct((subs, nb, rhs), F32),
            jax.ShapeDtypeStruct((subs, nb, co), BF16),
        ],
        compiler_params=params(),
        cost_estimate=pl.CostEstimate(
            flops=2 * subs * nb * nb * rhs, bytes_accessed=4 * 10**6, transcendentals=0
        ),
        name="neumann_half",
    )(*stay(prim_map, neumann, basis), residual, halo)


def coarse_kernel(own, core, z, turned, ring, twin, part, out, near, far):
    s = pl.program_id(0)
    face = far.shape[0]
    groups = ring.shape[0]
    at = lax.rem(z[0] - (own[s] >> 1) + groups, groups)
    solved = jnp.where((own[s] & 1) != core[0], twin[at].astype(F32), ring[at].astype(F32)).astype(BF16)
    found = part[0] + 0.5 * dot(turned[0], solved)
    out[0] = found

    @pl.when(s == 0)
    def _():
        near[...] = found[:face]

    @pl.when(s == pl.num_programs(0) - 1)
    def _():
        far[...] = found[face:]


def coarse_part(own, core, z, turned, ring, twin, part):
    subs, nb, co = turned.shape
    rhs = ring.shape[2]
    return pl.pallas_call(
        coarse_kernel,
        grid=(subs,),
        in_specs=[
            smem(),
            smem(),
            smem(),
            pl.BlockSpec((1, nb, co), lambda s: (s, 0, 0)),
            whole(ring.shape),
            whole(twin.shape),
            pl.BlockSpec((1, nb, rhs), lambda s: (s, 0, 0)),
        ],
        out_specs=[
            pl.BlockSpec((1, nb, rhs), lambda s: (s, 0, 0)),
            whole((nb // 2, rhs)),
            whole((nb // 2, rhs)),
        ],
        out_shape=[
            jax.ShapeDtypeStruct((subs, nb, rhs), F32),
            jax.ShapeDtypeStruct((nb // 2, rhs), F32),
            jax.ShapeDtypeStruct((nb // 2, rhs), F32),
        ],
        compiler_params=params(),
        name="coarse_part",
    )(own, core, z, turned, ring, twin, part)


def action(stiffness, coupling, interior, field):
    across = field.T.astype(BF16)
    load = dot(across, coupling).astype(BF16)
    inside = dot(load, interior, NT).astype(BF16)
    return dot(stiffness, field.astype(BF16)) - dot(coupling, inside, NT)


def cost(steps, nb, ni, rhs):
    return pl.CostEstimate(
        flops=2 * steps * rhs * (nb * nb + 2 * nb * ni + ni * ni),
        bytes_accessed=2 * steps * (nb * nb + nb * ni + ni * ni),
        transcendentals=0,
    )


def act(stiffness, coupling, interior, own_p, far_p, own_d, far_d, own_r):
    face, rhs = own_p.shape
    field = jnp.concatenate(
        [jnp.concatenate([own_p, own_d], axis=1), jnp.concatenate([far_p, far_d], axis=1)], axis=0
    )
    both = action(stiffness[0], coupling[0], interior[0], field)
    image, moved = both[:, :rhs], both[:, rhs:]
    parts = jnp.concatenate(
        [
            column_sum(own_r * own_p),
            column_sum(own_p * image[:face] + far_p * image[face:]),
            column_sum(own_p * moved[:face] + far_p * moved[face:])
            + column_sum(own_d * image[:face] + far_d * image[face:]),
            column_sum(own_d * moved[:face] + far_d * moved[face:]),
        ],
        axis=0,
    )
    return both, parts


def inner_kernel(
    coupling, interior, stiffness, near_p, far_p, behind_p, ahead_p, own_d, far_d, own_r, *rest
):
    sources, (out, sums), places, sems = rest[:3], rest[3:5], rest[5:8], rest[8]
    i = pl.program_id(0)
    copies = fetches((0, sources[0].shape[0] - 1), sources, places, sems)

    @pl.when(i == 0)
    def _():
        for copy in copies:
            copy.start()

    out[0], parts = act(
        stiffness,
        coupling,
        interior,
        near_p[0] + behind_p[0],
        ahead_p[0] + far_p[0],
        own_d[0],
        far_d[0],
        own_r[0],
    )

    @pl.when(i == 0)
    def _():
        sums[...] = parts

    @pl.when(i > 0)
    def _():
        sums[...] += parts
        for copy in copies:
            copy.wait()


def outer_kernel(
    coupling,
    interior,
    stiffness,
    near_p,
    far_p,
    behind_p,
    ahead_p,
    own_d,
    far_d,
    own_r,
    from_prev,
    from_next,
    direction_halo,
    earlier,
    out,
    copies,
    far,
    sums,
):
    i = pl.program_id(0)
    face = far.shape[0]
    own = near_p[0] + jnp.where(i == 0, from_prev[...], behind_p[0])
    after = far_p[0] + jnp.where(i == 0, ahead_p[0], from_next[...])
    after_d = jnp.where(i == 0, far_d[0], direction_halo[...])
    both, parts = act(stiffness, coupling, interior, own, after, own_d[0], after_d, own_r[0])
    out[0] = both

    @pl.when(i == 0)
    def _():
        sums[...] = earlier[...] + parts

    @pl.when(i > 0)
    def _():
        far[...] = both[face:]
        total = sums[...] + parts
        for k in range(copies.shape[0]):
            copies[k] = total


def search(kernel, name, first, stride, extra, scratch, held, pre, direction, residual, *rest, ahead=()):
    _, nb, ni = held[0].shape
    subs = direction.shape[0]
    rhs = direction.shape[2]
    face = nb // 2
    last = subs - 1

    def block(shape, shift=0, half=0):
        def place(i):
            s = first + stride * i + shift
            return (jnp.minimum(jnp.maximum(s, 0), last), half, 0)

        return pl.BlockSpec((1,) + shape, place)

    def operator(shape):
        if held[0].shape[0] == subs:
            return block(shape)
        return pl.BlockSpec((1,) + shape, lambda i: (i, 0, 0))

    faces = (face, rhs)
    return pl.pallas_call(
        kernel,
        grid=(2,),
        in_specs=[
            operator((nb, ni)),
            operator((ni, ni)),
            operator((nb, nb)),
            block(faces),
            block(faces, 0, 1),
            block(faces, -1, 1),
            block(faces, 1, 0),
            block(faces),
            block(faces, 1),
            block(faces),
        ]
        + [whole(x.shape) for x in rest]
        + [IN_HBM for _ in ahead],
        out_specs=[pl.BlockSpec((1, nb, 2 * rhs), lambda i: (i, 0, 0))]
        + [whole(x) for x in extra]
        + [ANYWHERE for _ in ahead],
        out_shape=[jax.ShapeDtypeStruct((2, nb, 2 * rhs), F32)]
        + [jax.ShapeDtypeStruct(x, F32) for x in extra]
        + fetched(ahead),
        scratch_shapes=scratch,
        compiler_params=params(LARGE),
        cost_estimate=cost(2, nb, ni, 2 * rhs),
        name=name,
    )(
        *held,
        pre,
        pre,
        pre,
        pre,
        direction,
        direction,
        residual,
        *rest,
        *stay(*ahead),
    )


def update_kernel(
    sums, last_inner, pre, from_prev, outer, inside, before, direction, residual, solution, new_sol, new_res
):
    total = jnp.sum(sums[...], axis=0)
    inner = total[0:1]
    beta = inner / last_inner[...]
    curvature = total[1:2] + beta * (total[2:3] + beta * total[3:4])
    step = inner / curvature
    subs, face, rhs = direction.shape
    last = subs - 1

    def part(s):
        return outer[0] if s == 0 else outer[1] if s == last else inside[s - 1]

    for s in range(subs):
        behind = from_prev[...] if s == 0 else pre[s - 1, face:]
        both = part(s)[:face] + (before[...] if s == 0 else part(s - 1)[face:])
        search = pre[s, :face] + behind + beta * direction[s]
        image = both[:, :rhs] + beta * both[:, rhs:]
        new_sol[s] = solution[s] + step * search
        new_res[s] = residual[s] - step * image


def update(*args):
    shape = jax.ShapeDtypeStruct(args[-1].shape, F32)
    return pl.pallas_call(
        update_kernel, out_shape=[shape, shape], compiler_params=params(), name="update"
    )(*args)


def local(
    solution,
    residual,
    direction,
    last_inner,
    stiffness,
    coupling,
    interior,
    neumann,
    basis,
    panels,
    base_coarse,
    owners,
    prim_map,
    changed,
):
    groups = lax.axis_size("z")
    pieces = lax.axis_size("narrow")
    devices = groups * 2 * pieces
    face, rhs = residual.shape[1:]
    forward = [(i, (i + 1) % pieces) for i in range(pieces)]
    back = [((i + 1) % pieces, i) for i in range(pieces)]
    own = owners[:, 0]
    core = lax.axis_index("core")
    core_ref = core.astype(jnp.int32).reshape(1)
    z_ref = lax.axis_index("z").astype(jnp.int32).reshape(1)

    halo = lax.ppermute(residual[0].astype(BF16), "narrow", back)
    basis = jnp.swapaxes(basis, 1, 2)
    keep, send, edge = place_panels(own, changed, core_ref, prim_map, basis, panels, residual, groups)
    keep, send = add_halo(own, core_ref, edge, halo, keep, send)
    mine = keep + lax.ppermute(send, "core", [(0, 1), (1, 0)])
    rows = mine.shape[1] // pieces
    parts = lax.all_to_all(
        mine.reshape(groups * pieces, rows, rhs), ("z", "narrow"), 0, 0, tiled=True
    )
    copies = sum_copies(parts, pieces)
    packed = lax.all_to_all(copies, "narrow", 0, 0, tiled=True)
    solved = solve_block(packed.reshape(pieces * rows, rhs), base_coarse)

    turns = [lax.ppermute(solved, "z", [(i, (i + d) % groups) for i in range(groups)]) for d in range(1, groups)]
    given, heading, _ = lax.optimization_barrier((residual, direction[0], solved))
    direction_halo = lax.ppermute(heading, "narrow", back)
    part, turned = neumann_half(prim_map, neumann, basis, given, halo)
    turns, part, turned = lax.optimization_barrier((turns, part, turned))
    ring = jnp.stack([solved] + turns)
    twin = lax.ppermute(ring, "core", [(0, 1), (1, 0)])
    pre, near, far = coarse_part(own, core_ref, z_ref, turned, ring, twin, part)
    from_prev = lax.ppermute(far, "narrow", forward)
    from_next = lax.ppermute(near, "narrow", back)
    subs, nb, _ = coupling.shape
    operators = (coupling, interior, stiffness)
    mine = (pre, direction, residual)
    inside, sums, *other = search(
        inner_kernel,
        "search_inner",
        1,
        1,
        [(4, rhs)],
        [pltpu.SemaphoreType.DMA((3, 2))],
        stay(*operators),
        *mine,
        ahead=operators,
    )
    outer, sums, behind = search(
        outer_kernel,
        "search_outer",
        0,
        subs - 1,
        [(devices, 4, rhs), (nb // 2, 2 * rhs)],
        [pltpu.VMEM((4, rhs), F32)],
        other,
        *mine,
        from_prev,
        from_next,
        direction_halo,
        sums,
    )
    before = lax.ppermute(behind, "narrow", forward)
    sums = lax.all_to_all(sums, ("z", "core", "narrow"), 0, 0, tiled=True)
    return tuple(
        update(
            sums,
            last_inner[None],
            pre,
            from_prev,
            outer,
            inside,
            before,
            direction,
            residual,
            solution,
        )
    )


def solution(mesh):
    wide, narrow = mesh.devices.shape
    finer = Mesh(mesh.devices.reshape(wide // 2, 2, narrow), ("z", "core", "narrow"))
    split = ("z", "core", "narrow")
    in_specs = (
        P(split, None, None),
        P(split, None, None),
        P(split, None, None),
        P(),
        P(split, None, None),
        P(split, None, None),
        P(split, None, None),
        P(split, None, None),
        P(split, None, None),
        P(split, None, None),
        P(("z", "core"), None, None),
        P(split, None),
        P(split, None),
        P(split),
    )
    out_specs = (P(split, None, None), P(split, None, None))
    return jax.shard_map(local, mesh=finer, in_specs=in_specs, out_specs=out_specs, check_vma=False)
```

```python
import jax
import jax.numpy as jnp
from jax import lax
from jax.experimental import pallas as pl
from jax.experimental.pallas import tpu as pltpu
from jax.sharding import Mesh, PartitionSpec as P

F32 = jnp.float32
BF16 = jnp.bfloat16
NN = (((1,), (0,)), ((), ()))
NT = (((1,), (1,)), ((), ()))
TN = (((0,), (0,)), ((), ()))
SMALL = 16 * 1024 * 1024
LARGE = 24 * 1024 * 1024
PLACE = 16 * 1024 * 1024
HIGHEST = lax.Precision.HIGHEST


def dot(a, b, dims=NN, precision=None):
    return lax.dot_general(a, b, dims, precision=precision, preferred_element_type=F32)


def smem():
    return pl.BlockSpec(memory_space=pltpu.SMEM)


def whole(shape):
    return pl.BlockSpec(shape, lambda *_: (0,) * len(shape))


def params(limit=SMALL):
    return pltpu.CompilerParams(vmem_limit_bytes=limit)


def stay(*arrays):
    return tuple(pltpu.with_memory_space_constraint(x, pltpu.HBM) for x in arrays)


def column_sum(value):
    return jnp.sum(value, axis=0, keepdims=True)


def chosen(pm, s, co):
    rows = lax.broadcasted_iota(jnp.int32, (co, pm.shape[1]), 0)
    return (rows == pm[pl.ds(s, 1)]).astype(F32).astype(BF16)


def place_kernel(own, chg, core, pm, basis, panel, res, keep, send, edge, held, sems):
    s = pl.program_id(0)
    last = pl.num_programs(0) - 1
    co = edge.shape[0]
    half = co // 2
    face = res.shape[1]

    @pl.when(s == 0)
    def _():
        held[...] = jnp.zeros_like(held)

    select = chosen(pm, s, co)
    wide_basis = dot(select, basis[0]).astype(BF16)
    placed = dot(dot(select, panel[0]).astype(BF16), select, NT) * chg[s].astype(F32)
    here = res[s].astype(BF16)
    there = res[jnp.minimum(s + 1, last)].astype(BF16)
    rhs = dot(wide_basis[:, :face], here)
    rhs += jnp.where(s < last, dot(wide_basis[:, face:], there), 0.0)
    owner = own[s]
    place = owner >> 1
    leaves = (owner & 1) ^ core[0]
    held[leaves, place, 0:half] += placed[:half, :half]
    held[leaves, place, half:co] += placed[half:, :half]
    held[leaves, place, co : co + half] += placed[half:, half:]
    held[leaves, place, co + half :] += rhs

    @pl.when(s == last)
    def _():
        edge[...] = wide_basis[:, face:]
        first = pltpu.make_async_copy(held.at[1], send, sems.at[0])
        second = pltpu.make_async_copy(held.at[0], keep, sems.at[1])
        first.start()
        second.start()
        first.wait()
        second.wait()


def place_panels(own, chg, core, prim_map, basis, panels, residual, groups):
    subs, npr, nb = basis.shape
    co = 2 * residual.shape[2]
    rows = 3 * (co // 2) + co
    packed = (groups, rows, co // 2)
    hbm = pl.BlockSpec(memory_space=pl.ANY)
    return pl.pallas_call(
        place_kernel,
        grid=(subs,),
        in_specs=[
            smem(),
            smem(),
            smem(),
            whole((subs, npr)),
            pl.BlockSpec((1, npr, nb), lambda s: (s, 0, 0)),
            pl.BlockSpec((1, npr, npr), lambda s: (s, 0, 0)),
            whole(residual.shape),
        ],
        out_specs=[hbm, hbm, whole((co, nb // 2))],
        out_shape=[
            jax.ShapeDtypeStruct(packed, F32),
            jax.ShapeDtypeStruct(packed, F32),
            jax.ShapeDtypeStruct((co, nb // 2), BF16),
        ],
        scratch_shapes=[pltpu.VMEM((2,) + packed, F32), pltpu.SemaphoreType.DMA((2,))],
        compiler_params=params(PLACE),
        cost_estimate=pl.CostEstimate(flops=10**9, bytes_accessed=6 * 10**6, transcendentals=0),
        name="place_panels",
    )(*stay(own, chg), core, *stay(prim_map, basis, panels, residual))


def halo_kernel(own, core, edge, halo, keep_in, send_in, keep, send, held, sem):
    del keep_in, send_in
    owner = own[own.shape[0] - 1]
    place = owner >> 1
    other = (owner & 1) != core[0]
    rows = held.shape[0]

    def add(to):
        part = to.at[place, pl.ds(to.shape[1] - rows, rows)]
        fetch = pltpu.make_async_copy(part, held, sem)
        fetch.start()
        value = dot(edge[...], halo[...])
        fetch.wait()
        held[...] += value
        put = pltpu.make_async_copy(held, part, sem)
        put.start()
        put.wait()

    @pl.when(other)
    def _():
        add(send)

    @pl.when(jnp.logical_not(other))
    def _():
        add(keep)


def add_halo(own, core, edge, halo, keep, send):
    hbm = pl.BlockSpec(memory_space=pl.ANY)
    return pl.pallas_call(
        halo_kernel,
        grid=(1,),
        in_specs=[
            smem(),
            smem(),
            whole(edge.shape),
            whole(halo.shape),
            hbm,
            hbm,
        ],
        out_specs=[hbm, hbm],
        out_shape=[jax.ShapeDtypeStruct(keep.shape, F32), jax.ShapeDtypeStruct(send.shape, F32)],
        input_output_aliases={4: 0, 5: 1},
        scratch_shapes=[pltpu.VMEM((edge.shape[0], halo.shape[1]), F32), pltpu.SemaphoreType.DMA],
        compiler_params=params(PLACE),
        name="add_halo",
    )(own, core, edge, halo, keep, send)


def gather_kernel(parts, out):
    total = jnp.sum(parts[...], axis=0)
    for i in range(out.shape[0]):
        out[i] = total


def sum_copies(parts, copies):
    return pl.pallas_call(
        gather_kernel,
        out_shape=jax.ShapeDtypeStruct((copies,) + parts.shape[1:], F32),
        compiler_params=params(),
        name="sum_copies",
    )(parts)


MOST_STEPS = 24


def inverse(matrix):
    n = matrix.shape[0]
    lanes = lax.broadcasted_iota(jnp.int32, (8, n), 1)
    subl = lax.broadcasted_iota(jnp.int32, (8, n), 0)
    tiles = tuple(matrix[8 * i : 8 * i + 8] for i in range(n // 8))

    def group(_, tiles):
        tiles = list(tiles)
        for j in range(8):
            pivot_row = tiles[0][j : j + 1, :]
            scale = 1.0 / pivot_row[:, j : j + 1]
            row = jnp.where(lanes[:1] == j, scale, pivot_row * scale)
            for i, tile in enumerate(tiles):
                new = jnp.where(lanes == j, 0.0, tile) - tile[:, j : j + 1] * row
                if i == 0:
                    new = jnp.where(subl == j, row, new)
                tiles[i] = new
        return tuple(pltpu.roll(tile, n - 8, 1) for tile in tiles[1:] + tiles[:1])

    return jnp.concatenate(lax.fori_loop(0, n // 8, group, tiles), axis=0)


def split(value, terms):
    found = []
    for _ in range(terms):
        found.append(value.astype(BF16))
        value = value - found[-1].astype(F32)
    return found


def eliminate(matrix, right):
    half = matrix.shape[0] // 2
    a21 = matrix[half:, :half]
    b1, b2 = right[:half], right[half:]
    inv1 = inverse(matrix[:half, :half])
    carry = dot(a21, inv1, NN, HIGHEST)
    inv2 = inverse(matrix[half:, half:] - dot(carry, a21, NT, HIGHEST))
    x2 = dot(inv2, b2 - dot(carry, b1, NN, HIGHEST), NN, HIGHEST)
    x1 = dot(inv1, b1, NN, HIGHEST) - dot(carry, x2, TN, HIGHEST)
    return x1, x2


def solve_kernel(packed, base, out, mat, terms, x, r, p):
    co = out.shape[0]
    half = co // 2
    a21 = packed[half:co]
    mat[:half, :half] = packed[:half] + base[0, :half, :half]
    mat[half:, :half] = a21 + base[0, half:, :half]
    mat[:half, half:] = a21.T + base[0, :half, half:]
    mat[half:, half:] = packed[co : co + half] + base[0, half:, half:]
    rows = lax.broadcasted_iota(jnp.int32, (co, co), 0)
    columns = lax.broadcasted_iota(jnp.int32, (co, co), 1)
    scale = 1.0 / jnp.sum(jnp.where(rows == columns, mat[...], 0.0), axis=1, keepdims=True)
    for i, term in enumerate(split(mat[...], 3)):
        terms[i] = term
    right = packed[co + half :]
    size = jnp.max(jnp.abs(right), axis=0, keepdims=True)
    size = jnp.where(size > 0.0, size, 1.0)
    right = right * (1.0 / size)

    def times(value):
        n = value.shape[1]
        v1, v2, v3 = split(value, 3)
        pair = jnp.concatenate([v1, v2], axis=1)
        first = dot(terms[0], pair)
        second = dot(terms[1], pair)
        small = second[:, n:] + dot(terms[0], v3) + dot(terms[2], v1)
        return first[:, :n] + (first[:, n:] + second[:, :n] + small)

    x[...] = jnp.zeros_like(right)
    r[...] = right
    p[...] = scale * right
    start = column_sum(right * (scale * right))

    def steps(state):
        count, norm, _ = state
        for _ in range(2):
            image = times(p[...])
            energy = column_sum(p[...] * image)
            length = jnp.where(energy > 0.0, norm / energy, 0.0)
            x[...] += length * p[...]
            left = r[...] - length * image
            r[...] = left
            scaled = scale * left
            new = column_sum(left * scaled)
            p[...] = scaled + jnp.where(norm > 0.0, new / norm, 0.0) * p[...]
            norm = new
        return count + 2, norm, jnp.max(norm - 1e-12 * start) > 0.0

    lax.while_loop(
        lambda state: state[2] & (state[0] < MOST_STEPS), steps, (jnp.int32(0), start, jnp.bool_(True))
    )
    left = right - dot(mat[...], x[...], NN, HIGHEST)
    solved = jnp.max(column_sum(left * (scale * left)) - 1e-11 * start) <= 0.0

    @pl.when(solved)
    def _():
        out[...] = (x[...] * size).astype(BF16)

    @pl.when(jnp.logical_not(solved))
    def _():
        x1, x2 = eliminate(mat[...], packed[co + half :])
        out[:half] = x1.astype(BF16)
        out[half:] = x2.astype(BF16)


def solve_block(packed, base):
    co = base.shape[1]
    rhs = packed.shape[1]
    return pl.pallas_call(
        solve_kernel,
        out_shape=jax.ShapeDtypeStruct((co, rhs), BF16),
        scratch_shapes=[
            pltpu.VMEM((co, co), F32),
            pltpu.VMEM((3, co, co), BF16),
            pltpu.VMEM((co, rhs), F32),
            pltpu.VMEM((co, rhs), F32),
            pltpu.VMEM((co, rhs), F32),
        ],
        compiler_params=params(),
        name="solve_block",
    )(packed, base)


def fetches(subs, sources, places, sems):
    return [
        pltpu.make_async_copy(source.at[s], place.at[j], sems.at[k, j])
        for k, (source, place) in enumerate(zip(sources, places))
        for j, s in enumerate(subs)
    ]


def fetched(operators):
    return [jax.ShapeDtypeStruct((2,) + x.shape[1:], x.dtype) for x in operators]


ANYWHERE = pl.BlockSpec(memory_space=pl.ANY)
IN_HBM = pl.BlockSpec(memory_space=pltpu.HBM)


def neumann_kernel(pm, neumann, basis, res, halo, out, turned):
    s = pl.program_id(0)
    last = pl.num_programs(0) - 1
    here = res[s].astype(BF16)
    there = jnp.where(s < last, res[jnp.minimum(s + 1, last)], halo[...].astype(F32)).astype(BF16)
    out[0] = 0.5 * dot(neumann[0], jnp.concatenate([here, there], axis=0))
    turned[0] = dot(chosen(pm, s, turned.shape[2]), basis[0]).astype(BF16).T


def neumann_half(prim_map, neumann, basis, residual, halo):
    subs, npr, nb = basis.shape
    rhs = residual.shape[2]
    co = 2 * rhs
    return pl.pallas_call(
        neumann_kernel,
        grid=(subs,),
        in_specs=[
            whole((subs, npr)),
            pl.BlockSpec((1, nb, nb), lambda s: (s, 0, 0)),
            pl.BlockSpec((1, npr, nb), lambda s: (s, 0, 0)),
            whole(residual.shape),
            whole(halo.shape),
        ],
        out_specs=[
            pl.BlockSpec((1, nb, rhs), lambda s: (s, 0, 0)),
            pl.BlockSpec((1, nb, co), lambda s: (s, 0, 0)),
        ],
        out_shape=[
            jax.ShapeDtypeStruct((subs, nb, rhs), F32),
            jax.ShapeDtypeStruct((subs, nb, co), BF16),
        ],
        compiler_params=params(),
        cost_estimate=pl.CostEstimate(
            flops=2 * subs * nb * nb * rhs, bytes_accessed=4 * 10**6, transcendentals=0
        ),
        name="neumann_half",
    )(*stay(prim_map, neumann, basis), residual, halo)


def solution_of(s, own, core, z, ring, twin):
    groups = ring.shape[0]
    at = lax.rem(z[0] - (own[s] >> 1) + groups, groups)
    other = (own[s] & 1) != core[0]
    return jnp.where(other, twin[at].astype(F32), ring[at].astype(F32)).astype(BF16)


def coarse_kernel(own, core, z, turned, ring, twin, part, out):
    s = pl.program_id(0)
    out[0] = part[0] + 0.5 * dot(turned[0], solution_of(s, own, core, z, ring, twin))


def edge_kernel(own, core, z, turned, turned_last, ring, twin, part, part_last, near, far):
    last = own.shape[0] - 1
    near[...] = part[0] + 0.5 * dot(turned[0], solution_of(0, own, core, z, ring, twin))
    far[...] = part_last[0] + 0.5 * dot(
        turned_last[0], solution_of(last, own, core, z, ring, twin)
    )


def coarse_part(own, core, z, turned, ring, twin, part):
    subs, nb, co = turned.shape
    rhs = ring.shape[2]
    return pl.pallas_call(
        coarse_kernel,
        grid=(subs,),
        in_specs=[
            smem(),
            smem(),
            smem(),
            pl.BlockSpec((1, nb, co), lambda s: (s, 0, 0)),
            whole(ring.shape),
            whole(twin.shape),
            pl.BlockSpec((1, nb, rhs), lambda s: (s, 0, 0)),
        ],
        out_specs=pl.BlockSpec((1, nb, rhs), lambda s: (s, 0, 0)),
        out_shape=jax.ShapeDtypeStruct((subs, nb, rhs), F32),
        compiler_params=params(),
        name="coarse_part",
    )(own, core, z, turned, ring, twin, part)


def coarse_edges(own, core, z, turned, ring, twin, part):
    subs, nb, co = turned.shape
    rhs = ring.shape[2]
    face = nb // 2
    shape = jax.ShapeDtypeStruct((face, rhs), F32)
    return pl.pallas_call(
        edge_kernel,
        grid=(1,),
        in_specs=[
            smem(),
            smem(),
            smem(),
            pl.BlockSpec((1, face, co), lambda _: (0, 0, 0)),
            pl.BlockSpec((1, face, co), lambda _: (subs - 1, 1, 0)),
            whole(ring.shape),
            whole(twin.shape),
            pl.BlockSpec((1, face, rhs), lambda _: (0, 0, 0)),
            pl.BlockSpec((1, face, rhs), lambda _: (subs - 1, 1, 0)),
        ],
        out_specs=[whole((face, rhs)), whole((face, rhs))],
        out_shape=[shape, shape],
        compiler_params=params(),
        name="coarse_edges",
    )(own, core, z, turned, turned, ring, twin, part, part)


def action(stiffness, coupling, interior, field):
    across = field.T.astype(BF16)
    load = dot(across, coupling).astype(BF16)
    inside = dot(load, interior, NT).astype(BF16)
    return dot(stiffness, field.astype(BF16)) - dot(coupling, inside, NT)


def cost(steps, nb, ni, rhs):
    return pl.CostEstimate(
        flops=2 * steps * rhs * (nb * nb + 2 * nb * ni + ni * ni),
        bytes_accessed=2 * steps * (nb * nb + nb * ni + ni * ni),
        transcendentals=0,
    )


def act(stiffness, coupling, interior, own_p, far_p, own_d, far_d, own_r):
    face, rhs = own_p.shape
    field = jnp.concatenate(
        [jnp.concatenate([own_p, own_d], axis=1), jnp.concatenate([far_p, far_d], axis=1)], axis=0
    )
    both = action(stiffness[0], coupling[0], interior[0], field)
    image, moved = both[:, :rhs], both[:, rhs:]
    parts = jnp.concatenate(
        [
            column_sum(own_r * own_p),
            column_sum(own_p * image[:face] + far_p * image[face:]),
            column_sum(own_p * moved[:face] + far_p * moved[face:])
            + column_sum(own_d * image[:face] + far_d * image[face:]),
            column_sum(own_d * moved[:face] + far_d * moved[face:]),
        ],
        axis=0,
    )
    return both, parts


def inner_kernel(
    coupling, interior, stiffness, near_p, far_p, behind_p, ahead_p, own_d, far_d, own_r, *rest
):
    sources, (out, sums), places, sems = rest[:3], rest[3:5], rest[5:8], rest[8]
    i = pl.program_id(0)
    copies = fetches((0, sources[0].shape[0] - 1), sources, places, sems)

    @pl.when(i == 0)
    def _():
        for copy in copies:
            copy.start()

    out[0], parts = act(
        stiffness,
        coupling,
        interior,
        near_p[0] + behind_p[0],
        ahead_p[0] + far_p[0],
        own_d[0],
        far_d[0],
        own_r[0],
    )

    @pl.when(i == 0)
    def _():
        sums[...] = parts

    @pl.when(i > 0)
    def _():
        sums[...] += parts
        for copy in copies:
            copy.wait()


def outer_kernel(
    coupling,
    interior,
    stiffness,
    near_p,
    far_p,
    behind_p,
    ahead_p,
    own_d,
    far_d,
    own_r,
    from_prev,
    from_next,
    direction_halo,
    earlier,
    out,
    copies,
    far,
    sums,
):
    i = pl.program_id(0)
    face = far.shape[0]
    own = near_p[0] + jnp.where(i == 0, from_prev[...], behind_p[0])
    after = far_p[0] + jnp.where(i == 0, ahead_p[0], from_next[...])
    after_d = jnp.where(i == 0, far_d[0], direction_halo[...])
    both, parts = act(stiffness, coupling, interior, own, after, own_d[0], after_d, own_r[0])
    out[0] = both

    @pl.when(i == 0)
    def _():
        sums[...] = earlier[...] + parts

    @pl.when(i > 0)
    def _():
        far[...] = both[face:]
        total = sums[...] + parts
        for k in range(copies.shape[0]):
            copies[k] = total


def search(kernel, name, first, stride, extra, scratch, held, pre, direction, residual, *rest, ahead=()):
    _, nb, ni = held[0].shape
    subs = direction.shape[0]
    rhs = direction.shape[2]
    face = nb // 2
    last = subs - 1

    def block(shape, shift=0, half=0):
        def place(i):
            s = first + stride * i + shift
            return (jnp.minimum(jnp.maximum(s, 0), last), half, 0)

        return pl.BlockSpec((1,) + shape, place)

    def operator(shape):
        if held[0].shape[0] == subs:
            return block(shape)
        return pl.BlockSpec((1,) + shape, lambda i: (i, 0, 0))

    faces = (face, rhs)
    return pl.pallas_call(
        kernel,
        grid=(2,),
        in_specs=[
            operator((nb, ni)),
            operator((ni, ni)),
            operator((nb, nb)),
            block(faces),
            block(faces, 0, 1),
            block(faces, -1, 1),
            block(faces, 1, 0),
            block(faces),
            block(faces, 1),
            block(faces),
        ]
        + [whole(x.shape) for x in rest]
        + [IN_HBM for _ in ahead],
        out_specs=[pl.BlockSpec((1, nb, 2 * rhs), lambda i: (i, 0, 0))]
        + [whole(x) for x in extra]
        + [ANYWHERE for _ in ahead],
        out_shape=[jax.ShapeDtypeStruct((2, nb, 2 * rhs), F32)]
        + [jax.ShapeDtypeStruct(x, F32) for x in extra]
        + fetched(ahead),
        scratch_shapes=scratch,
        compiler_params=params(LARGE),
        cost_estimate=cost(2, nb, ni, 2 * rhs),
        name=name,
    )(
        *held,
        pre,
        pre,
        pre,
        pre,
        direction,
        direction,
        residual,
        *rest,
        *stay(*ahead),
    )


def update_kernel(
    sums, last_inner, pre, from_prev, outer, inside, before, direction, residual, solution, new_sol, new_res
):
    total = jnp.sum(sums[...], axis=0)
    inner = total[0:1]
    beta = inner / last_inner[...]
    curvature = total[1:2] + beta * (total[2:3] + beta * total[3:4])
    step = inner / curvature
    subs, face, rhs = direction.shape
    last = subs - 1

    def part(s):
        return outer[0] if s == 0 else outer[1] if s == last else inside[s - 1]

    for s in range(subs):
        behind = from_prev[...] if s == 0 else pre[s - 1, face:]
        both = part(s)[:face] + (before[...] if s == 0 else part(s - 1)[face:])
        search = pre[s, :face] + behind + beta * direction[s]
        image = both[:, :rhs] + beta * both[:, rhs:]
        new_sol[s] = solution[s] + step * search
        new_res[s] = residual[s] - step * image


def update(*args):
    shape = jax.ShapeDtypeStruct(args[-1].shape, F32)
    return pl.pallas_call(
        update_kernel, out_shape=[shape, shape], compiler_params=params(), name="update"
    )(*args)


def local(
    solution,
    residual,
    direction,
    last_inner,
    stiffness,
    coupling,
    interior,
    neumann,
    basis,
    panels,
    base_coarse,
    owners,
    prim_map,
    changed,
):
    groups = lax.axis_size("z")
    pieces = lax.axis_size("narrow")
    devices = groups * 2 * pieces
    face, rhs = residual.shape[1:]
    forward = [(i, (i + 1) % pieces) for i in range(pieces)]
    back = [((i + 1) % pieces, i) for i in range(pieces)]
    own = owners[:, 0]
    core = lax.axis_index("core")
    core_ref = core.astype(jnp.int32).reshape(1)
    z_ref = lax.axis_index("z").astype(jnp.int32).reshape(1)

    halo = lax.ppermute(residual[0].astype(BF16), "narrow", back)
    basis = jnp.swapaxes(basis, 1, 2)
    keep, send, edge = place_panels(own, changed, core_ref, prim_map, basis, panels, residual, groups)
    keep, send = add_halo(own, core_ref, edge, halo, keep, send)
    mine = keep + lax.ppermute(send, "core", [(0, 1), (1, 0)])
    rows = mine.shape[1] // pieces
    parts = lax.all_to_all(
        mine.reshape(groups * pieces, rows, rhs), ("z", "narrow"), 0, 0, tiled=True
    )
    copies = sum_copies(parts, pieces)
    packed = lax.all_to_all(copies, "narrow", 0, 0, tiled=True)
    solved = solve_block(packed.reshape(pieces * rows, rhs), base_coarse)

    turns = [lax.ppermute(solved, "z", [(i, (i + d) % groups) for i in range(groups)]) for d in range(1, groups)]
    given, heading, _ = lax.optimization_barrier((residual, direction[0], solved))
    direction_halo = lax.ppermute(heading, "narrow", back)
    part, turned = neumann_half(prim_map, neumann, basis, given, halo)
    turns, part, turned = lax.optimization_barrier((turns, part, turned))
    ring = jnp.stack([solved] + turns)
    twin = lax.ppermute(ring, "core", [(0, 1), (1, 0)])
    near, far = coarse_edges(own, core_ref, z_ref, turned, ring, twin, part)
    from_prev = lax.ppermute(far, "narrow", forward)
    from_next = lax.ppermute(near, "narrow", back)
    part, _, _ = lax.optimization_barrier((part, near, far))
    pre = coarse_part(own, core_ref, z_ref, turned, ring, twin, part)
    subs, nb, _ = coupling.shape
    operators = (coupling, interior, stiffness)
    mine = (pre, direction, residual)
    inside, sums, *other = search(
        inner_kernel,
        "search_inner",
        1,
        1,
        [(4, rhs)],
        [pltpu.SemaphoreType.DMA((3, 2))],
        stay(*operators),
        *mine,
        ahead=operators,
    )
    outer, sums, behind = search(
        outer_kernel,
        "search_outer",
        0,
        subs - 1,
        [(devices, 4, rhs), (nb // 2, 2 * rhs)],
        [pltpu.VMEM((4, rhs), F32)],
        other,
        *mine,
        from_prev,
        from_next,
        direction_halo,
        sums,
    )
    before = lax.ppermute(behind, "narrow", forward)
    sums = lax.all_to_all(sums, ("z", "core", "narrow"), 0, 0, tiled=True)
    return tuple(
        update(
            sums,
            last_inner[None],
            pre,
            from_prev,
            outer,
            inside,
            before,
            direction,
            residual,
            solution,
        )
    )


def solution(mesh):
    wide, narrow = mesh.devices.shape
    finer = Mesh(mesh.devices.reshape(wide // 2, 2, narrow), ("z", "core", "narrow"))
    split = ("z", "core", "narrow")
    in_specs = (
        P(split, None, None),
        P(split, None, None),
        P(split, None, None),
        P(),
        P(split, None, None),
        P(split, None, None),
        P(split, None, None),
        P(split, None, None),
        P(split, None, None),
        P(split, None, None),
        P(("z", "core"), None, None),
        P(split, None),
        P(split, None),
        P(split),
    )
    out_specs = (P(split, None, None), P(split, None, None))
    return jax.shard_map(local, mesh=finer, in_specs=in_specs, out_specs=out_specs, check_vma=False)
```
